32 devices in a mesh: groups: 2 (over y), adapter: 4 (over z), tensor: 2 (over x), section: 2 (over core).
Axes of the slice: x: 2, y: 2, z: 4, core: 2. Of those that a mesh axis runs over, the one named last changes fastest.
Arguments:
- activations: bfloat16 [1024, 8192], P(('groups', 'adapter', 'section'), 'tensor'), parts along dimension 0, may hold values from -6 to 6
- adapter_ids: int32 [1024, 1], P(('groups', 'adapter', 'section')), parts along dimension 0, may hold values from 0 to 7; in each aligned block of 64 rows (0 to 63, 64 to 127, ...) at most 16 rows name the same one
- base_weight: bfloat16 [8192, 8192], P('tensor', 'adapter'), may hold values from -0.0625 to 0.0625
- shrink_weight: bfloat16 [8, 8192, 64], P('adapter', 'tensor'), may hold values from -0.0625 to 0.0625
- expand_weight: bfloat16 [8, 64, 8192], P('adapter', None, 'tensor'), may hold values from -0.75 to 0.75
Outputs:
- projected: bfloat16 [1024, 8192], P(('groups', 'adapter', 'section'), 'tensor'), parts along dimension 0
The draws below stay inside these ranges and needn't reach their ends.
There are 2 independent parts, one for each index of `groups`. The reference program is written for one: setup_inputs(seed, part) draws one part's arguments, and reference() takes and returns one part's arrays. A program takes and returns all parts, laid end to end along the dimension named above; an argument that names none is the same for every part. Nothing has to cross between parts.
Inputs may be any that keep to these rules, and one draw needn't show every extreme that they name: `adapter_ids`: in each aligned block of 64 rows (the rows of one device), no adapter is named by more than 16 rows; in some blocks one adapter is named by exactly 16 rows.
All inputs are finite; a program needn't handle non-finite values.
Results may differ from the reference program's by a relative error of at most 0.0034.
Values may be sent and summed in bfloat16 or wider, within the bound.
No kernel may reach another device: no remote copies, remote signals or barrier semaphores. Data moves between devices by JAX's collectives and lax.ppermute only.
A program may use at most 64 MiB of HBM per device.

```python
import math
import jax
import jax.numpy as jnp
import numpy as np
from jax import lax

D = 8192
RANK = 64
TOK_DEV = 64
ADAPTERS = 8
MOST = 16
ROWS = 512


def block_levels(key, extent, pieces, low, largest):
    gain, own = 1.0, jax.random.fold_in(key, 6)
    for dim, shards_of in pieces:
        steps = jnp.exp(jax.random.uniform(jax.random.fold_in(own, dim), (shards_of,), jnp.float32, low / len(pieces), largest / len(pieces)))
        gain = gain * jnp.repeat(steps, extent[dim] // shards_of).reshape([-1 if axis == dim else 1 for axis in range(len(extent))])
    return gain


def assign_block(key, own, number, rows, count, top, most, slope):
    ranking = jax.random.permutation(key, count)
    heavy_load, ordinary = shares(count, rows * top, most, slope, True), shares(count, rows * top, most, slope, False)
    places = jnp.arange(count)

    def named(tallies, turn):
        used = int((tallies > 0).sum())
        fixed = max(1, used // 4)
        moved = fixed + (places - fixed + turn * (used - fixed)) % max(1, count - fixed)
        return jnp.zeros((count,), jnp.int32).at[ranking[jnp.where(places < fixed, places, moved)]].set(jnp.asarray(tallies, jnp.int32))

    tallies = jnp.where(number % 4 == 0, named(heavy_load, number // 4), named(ordinary, number - number // 4 - 1))
    mixed = jax.random.permutation(jax.random.fold_in(own, 3), count)
    donor, taker = mixed[0:count // 2 * 2:2], mixed[1:count // 2 * 2:2]
    room = jnp.minimum(tallies[donor] - 1, most - tallies[taker]) // 2
    room = jnp.where((donor == ranking[0]) | (taker == ranking[0]) | (tallies[taker] == 0), 0, jnp.maximum(room, 0))
    moved = jax.random.randint(jax.random.fold_in(own, 4), (count // 2,), 0, 1 << 20) % (room + 1)
    tallies = tallies.at[donor].add(-moved).at[taker].add(moved)
    items = jnp.searchsorted(jnp.cumsum(tallies), jnp.arange(rows * top), side="right").astype(jnp.int32)
    table = items.reshape(top, rows).T
    table = table[jax.random.permutation(jax.random.fold_in(own, 1), rows)]
    turn = jax.random.randint(jax.random.fold_in(own, 2), (rows, 1), 0, top)
    return jnp.take_along_axis(table, (jnp.arange(top)[None, :] + turn) % top, axis=1)


def shares(count, total, most, lean, full):
    loads = [(1 << 20) // math.isqrt(rank ** lean) + 1 for rank in range(1, count + 1)]
    largest = most if full else min(most, max(-(-total // count), total * loads[0] // sum(loads)))
    least = 1 if total - largest >= count - 1 else 0
    holding, spare = [largest] + [least] * (count - 1), total - largest - least * (count - 1)
    while spare > 0:
        movable = [i for i in range(1, count) if holding[i] < largest] or [i for i in range(1, count) if holding[i] < most]
        mass, remaining = sum([loads[i] for i in movable]), spare
        for i in movable:
            extra = min(most - holding[i], max(1, remaining * loads[i] // mass), spare)
            holding[i] = holding[i] + extra
            spare = spare - extra
    return np.array(holding)


def noise(rng, shape, deviation, reach, cuts=(), kind=jnp.bfloat16):
    array = deviation * jax.random.normal(rng, shape, jnp.float32)
    if cuts:
        array = array * block_levels(rng, shape, cuts, -0.22, 0.18)
    return jnp.clip(array, -reach, reach).astype(kind)


def setup_inputs(seed: int = 0, part: int = 0) -> dict:
    seeds = jax.random.split(jax.random.key(seed), 6)
    part_keys = jax.random.split(jax.random.fold_in(seeds[5], part), 6)
    activations = noise(part_keys[0], (ROWS, D), 1.0, 6.0, ((0, 8), (1, 2)))
    adapter_ids_keys = jax.random.split(jax.random.fold_in(part_keys[1], 1), ROWS // TOK_DEV)
    adapter_ids_turns = jax.random.permutation(jax.random.fold_in(part_keys[1], 3), ROWS // TOK_DEV)
    adapter_ids = jax.vmap(lambda own, number: assign_block(jax.random.fold_in(part_keys[1], 2), own, number, TOK_DEV, ADAPTERS, 1, MOST, 2))(adapter_ids_keys, adapter_ids_turns).reshape((ROWS, 1))
    base_weight = noise(seeds[2], (D, D), D ** -0.5, 0.0625, ((0, 2), (1, 4)))
    shrink_weight = noise(seeds[3], (ADAPTERS, D, RANK), D ** -0.5, 0.0625, ((0, 4), (1, 2)))
    expand_weight = noise(seeds[4], (ADAPTERS, RANK, D), RANK ** -0.5, 0.75, ((0, 4), (2, 2)))
    return {"activations": activations, "adapter_ids": adapter_ids, "base_weight": base_weight, "shrink_weight": shrink_weight, "expand_weight": expand_weight}


adapter_scale_factor = 0.5


def reference(activations, adapter_ids, base_weight, shrink_weight, expand_weight):
    base = jnp.dot(activations, base_weight, preferred_element_type=jnp.float32)
    row_ids = adapter_ids[:, 0].astype(jnp.int32)
    block_rows = activations.reshape(-1, 8, D)
    block_ids = row_ids.reshape(-1, 8)

    def one_block(pair):
        rows_here, ids_here = pair
        down_maps = shrink_weight[ids_here].astype(jnp.float32)
        shrunk = jnp.einsum("rd,rdk->rk", rows_here.astype(jnp.float32), down_maps).astype(jnp.bfloat16)
        up_maps = expand_weight[ids_here].astype(jnp.float32)
        expanded_rows = jnp.einsum("rk,rkn->rn", shrunk.astype(jnp.float32), up_maps)
        return (adapter_scale_factor * expanded_rows).astype(jnp.bfloat16)

    delta = lax.map(one_block, (block_rows, block_ids)).reshape(-1, D)
    return (base + delta.astype(jnp.float32)).astype(jnp.bfloat16)
```

```python
import functools

import jax
import jax.numpy as jnp
from jax import lax
from jax.experimental import pallas as pl
from jax.experimental.pallas import tpu as pltpu
from jax.sharding import PartitionSpec as P

adapter_scale_factor = 0.5
VMEM_LIMIT = 24 * 1024 * 1024


def ranks_of(block_ids):
    count = block_ids.shape[-1]
    earlier = lax.broadcasted_iota(jnp.int32, (count, count), 1) < lax.broadcasted_iota(
        jnp.int32, (count, count), 0
    )
    same = block_ids[..., :, None] == block_ids[..., None, :]
    return jnp.sum(jnp.logical_and(same, earlier).astype(jnp.int32), axis=-1)


def most_rows_of(tok_rows, adapters):
    return max(2, 2 * tok_rows // adapters)


def body_any(activations, adapter_ids, base_weight, shrink_weight, expand_weight):
    row_ids = adapter_ids[:, 0]
    tok_rows = activations.shape[0]
    feat_part = activations.shape[1]
    output_slice = expand_weight.shape[2]
    out_cols = base_weight.shape[1]
    n_adapt = lax.axis_size("adapter")
    local_count = shrink_weight.shape[0]
    most_rows = most_rows_of(tok_rows, local_count * n_adapt)
    resident_slot_list = local_count * most_rows
    all_slots = n_adapt * resident_slot_list
    home_slot = row_ids * most_rows + ranks_of(row_ids)
    home_map = (
        lax.broadcasted_iota(jnp.int32, (all_slots, tok_rows), 0) == home_slot[None, :]
    ).astype(jnp.bfloat16)
    base_part = jnp.dot(
        lax.all_gather(activations, "adapter", axis=0, tiled=True),
        base_weight,
        preferred_element_type=jnp.float32,
    )
    outgoing = jnp.dot(home_map, activations, preferred_element_type=jnp.float32).astype(
        jnp.bfloat16
    )
    outgoing = outgoing.reshape(n_adapt, resident_slot_list, feat_part)
    arrived = lax.all_to_all(outgoing, "adapter", split_axis=0, concat_axis=0, tiled=True)
    sender_slots = arrived.shape[0]
    grouped = arrived.reshape(sender_slots, local_count, most_rows, feat_part)
    partial_rank = jnp.einsum(
        "sjrd,jdk->sjrk", grouped, shrink_weight, preferred_element_type=jnp.float32
    )
    shrunk = lax.psum(partial_rank, "tensor").astype(jnp.bfloat16)
    expanded_rows = jnp.einsum(
        "sjrk,jkn->sjrn", shrunk, expand_weight, preferred_element_type=jnp.float32
    )
    final_outputs = (
        (adapter_scale_factor * expanded_rows)
        .astype(jnp.bfloat16)
        .reshape(sender_slots, resident_slot_list, output_slice)
    )
    returned = lax.all_to_all(final_outputs, "adapter", split_axis=0, concat_axis=0, tiled=True)
    delta = jnp.einsum(
        "st,sd->td",
        home_map,
        returned.reshape(all_slots, output_slice),
        preferred_element_type=jnp.float32,
    )
    base_blocks = base_part.reshape(n_adapt, tok_rows, out_cols)
    moved = lax.all_to_all(base_blocks, "adapter", split_axis=0, concat_axis=2, tiled=True)
    moved = moved.reshape(tok_rows, out_cols * n_adapt)
    base = lax.psum_scatter(moved, "tensor", scatter_dimension=1, tiled=True)
    return (base + delta).astype(jnp.bfloat16)


VM = pl.BlockSpec(memory_space=pltpu.VMEM)
SM = pl.BlockSpec(memory_space=pltpu.SMEM)
F32 = jnp.float32
BF16 = jnp.bfloat16


def stage_kernel(n_in, *refs):
    x_refs, (w_ref, s_ref, p32_ref, p16_ref, sh_ref) = refs[:n_in], refs[n_in:]
    x = x_refs[0][...]
    for other in x_refs[1:]:
        x = x + other[...]
    sh_ref[...] = lax.dot_general(
        x, s_ref[...], (((1,), (1,)), ((), ())), preferred_element_type=F32
    )
    cols = w_ref.shape[1]
    step = 256
    for j in range(0, cols, step):
        part = jnp.dot(x, w_ref[:, j : j + step], preferred_element_type=F32)
        p32_ref[:, j : j + step] = part
        p16_ref[:, j : j + step] = part.astype(BF16)


def stage(xs, w, s_t):
    rows, depth = xs[0].shape
    cols = w.shape[1]
    return pl.pallas_call(
        functools.partial(stage_kernel, len(xs)),
        in_specs=[VM] * (len(xs) + 2),
        out_specs=[VM] * 3,
        out_shape=[
            jax.ShapeDtypeStruct((rows, cols), F32),
            jax.ShapeDtypeStruct((rows, cols), BF16),
            jax.ShapeDtypeStruct((rows, s_t.shape[0]), F32),
        ],
        compiler_params=pltpu.CompilerParams(vmem_limit_bytes=VMEM_LIMIT),
        cost_estimate=pl.CostEstimate(
            flops=2 * rows * depth * cols, bytes_accessed=depth * cols * 2, transcendentals=0
        ),
    )(*xs, w, s_t)


def delta_kernel(k, most, meta_ref, slots_ref, e_ref, *refs):
    ins, outs = refs[: 2 * k], refs[2 * k :]
    local, rank, width = e_ref.shape
    first = meta_ref[0] * (local * most)
    table = slots_ref[...]
    which = lax.broadcasted_iota(jnp.int32, table.shape, 0)
    rows = table.shape[1]
    slot = lax.broadcasted_iota(jnp.int32, (local * most, rows), 0) + first
    for i in range(k):
        shrunk = (ins[2 * i][...] + ins[2 * i + 1][...]).astype(BF16)
        home = jnp.sum(jnp.where(which == meta_ref[1 + i], table, 0), axis=0, keepdims=True)
        pick = (slot == home).astype(BF16)
        chosen = jnp.dot(pick, shrunk, preferred_element_type=F32).astype(BF16)
        for j in range(local):
            lines = slice(j * most, (j + 1) * most)
            wide = jnp.dot(
                chosen[lines, j * rank : (j + 1) * rank], e_ref[j], preferred_element_type=F32
            )
            outs[i][lines, :] = (adapter_scale_factor * wide).astype(BF16)


def deltas(meta, slots, e, pairs, most):
    k = len(pairs)
    local, _, width = e.shape
    flat = [a for pair in pairs for a in pair]
    return pl.pallas_call(
        functools.partial(delta_kernel, k, most),
        in_specs=[SM] + [VM] * (2 + 2 * k),
        out_specs=[VM] * k,
        out_shape=[jax.ShapeDtypeStruct((local * most, width), BF16)] * k,
        compiler_params=pltpu.CompilerParams(vmem_limit_bytes=VMEM_LIMIT),
        cost_estimate=pl.CostEstimate(
            flops=k * 2 * local * most * 64 * width, bytes_accessed=4 << 20, transcendentals=0
        ),
    )(meta, slots, e, *flat)


def final_kernel(meta_ref, slot_ref, own32_ref, own16_ref, b1, b2, b3, d0, d1, d2, d3, o_ref, base):
    rows, quarter = own32_ref.shape
    spots = d0.shape[0]
    slot = slot_ref[...]
    lane = lax.broadcasted_iota(jnp.int32, (rows, spots), 1)
    picks = [(slot == lane + meta_ref[k] * spots).astype(BF16) for k in range(4)]
    for q in range(2):
        cols = slice(q * quarter, (q + 1) * quarter)
        source = meta_ref[4 + q]

        @pl.when(source == 0)
        def _():
            base[...] = own32_ref[...] + own16_ref[...].astype(F32)

        for k, ref in ((1, b1), (2, b2), (3, b3)):

            @pl.when(source == k)
            def _():
                base[...] = ref[...].astype(F32)

        total = base[...]
        for pick, d in zip(picks, (d0, d1, d2, d3)):
            total = total + jnp.dot(pick, d[:, cols], preferred_element_type=F32)
        o_ref[:, cols] = total.astype(BF16)


def body_four(activations, adapter_ids, base_weight, shrink_weight, expand_weight):
    row_ids = adapter_ids[:, 0]
    rows = activations.shape[0]
    local, _, rank = shrink_weight.shape
    quarter = base_weight.shape[1]
    most = most_rows_of(rows, local * 4)
    me = lax.axis_index("adapter")
    half = lax.axis_index("tensor")
    both = ("adapter", "tensor")

    def along(x, pairs):
        return lax.ppermute(x, "adapter", pairs)

    held = ((1, 3, 0, 2), (3, 2, 1, 0), (2, 0, 3, 1))

    def back(k):
        return [(a, held[k - 1][a]) for a in range(4)]

    def pick(table):
        return sum(jnp.where(me == a, table[a], 0) for a in range(4))

    planes = [[h for h in range(4)]]
    for k in (1, 2, 3):
        planes.append([held[k - 1].index(h) for h in range(4)])
    plane_of = [pick(p) for p in planes]
    source = [sum(jnp.where(plane_of[k] == 2 * half + q, k, 0) for k in range(4)) for q in (0, 1)]
    meta_home = jnp.stack(plane_of + source).astype(jnp.int32)
    meta_owner = jnp.stack([me, me] + [pick(h) for h in held]).astype(jnp.int32)

    home_slot = row_ids * most + ranks_of(row_ids)
    slots = lax.all_gather(home_slot[None, :], "adapter", axis=0, tiled=True)

    x = activations
    s_t = jnp.swapaxes(shrink_weight, 1, 2).reshape(local * rank, -1)
    w = base_weight
    got_a = along(x, [(0, 2), (3, 1), (1, 0), (2, 3)])
    p32_0, p16_0, s_0 = stage([x], w, s_t)
    x_later, p16_0 = lax.optimization_barrier((x, p16_0))
    got_c = along(x_later, [(0, 1), (3, 2), (2, 0), (1, 3)])
    got_b = along(x_later, [(1, 2), (2, 1)])
    got_f = along(got_a, [(1, 0), (2, 3)])

    p32_1, p16_1, s_1 = stage([got_a], w, s_t)
    p32_2, p16_2, s_2 = stage([got_f, got_b], w, s_t)
    p32_3, p16_3, s_3 = stage([got_c], w, s_t)

    def to_half(p):
        return lax.ppermute(
            p, both, [(2 * a + 1 - a // 2, 2 * a + a // 2) for a in range(4)]
        )

    def home_base(p, k):
        return lax.ppermute(
            p, both, [(2 * a + a // 2, 2 * h + a // 2) for a, h in back(k)]
        )

    def flip(s):
        return lax.ppermute(s, "tensor", [(0, 1), (1, 0)])

    own16 = to_half(p16_0)
    bases = []
    for k, p32, p16 in ((1, p32_1, p16_1), (2, p32_2, p16_2), (3, p32_3, p16_3)):
        bases.append(home_base((p32 + to_half(p16)).astype(BF16), k))

    e = expand_weight
    d_0, d_1 = deltas(meta_owner[0:3], slots, e, [(s_0, flip(s_0)), (s_1, flip(s_1))], most)
    (d_2,) = deltas(meta_owner[jnp.array([0, 3])], slots, e, [(s_2, flip(s_2))], most)
    (d_3,) = deltas(meta_owner[jnp.array([0, 4])], slots, e, [(s_3, flip(s_3))], most)
    d_1, d_2, d_3 = along(d_1, back(1)), along(d_2, back(2)), along(d_3, back(3))

    return pl.pallas_call(
        final_kernel,
        in_specs=[SM] + [VM] * 10,
        out_specs=VM,
        out_shape=jax.ShapeDtypeStruct((rows, 2 * quarter), BF16),
        scratch_shapes=[pltpu.VMEM((rows, quarter), F32)],
        compiler_params=pltpu.CompilerParams(vmem_limit_bytes=VMEM_LIMIT),
    )(meta_home, home_slot[:, None], p32_0, own16, *bases, d_0, d_1, d_2, d_3)


def solution(mesh):
    in_specs = (
        P(("groups", "adapter", "section"), "tensor"),
        P(("groups", "adapter", "section"), None),
        P("tensor", "adapter"),
        P("adapter", "tensor", None),
        P("adapter", None, "tensor"),
    )
    out_specs = P(("groups", "adapter", "section"), "tensor")
    four = mesh.shape["adapter"] == 4 and mesh.shape["tensor"] == 2
    body = body_four if four else body_any
    return jax.shard_map(body, mesh=mesh, in_specs=in_specs, out_specs=out_specs, check_vma=False)
```

```python
import functools

import jax
import jax.numpy as jnp
from jax import lax
from jax.experimental import pallas as pl
from jax.experimental.pallas import tpu as pltpu
from jax.sharding import PartitionSpec as P

adapter_scale_factor = 0.5
VMEM_LIMIT = 8 * 1024 * 1024


def ranks_of(block_ids):
    count = block_ids.shape[-1]
    earlier = lax.broadcasted_iota(jnp.int32, (count, count), 1) < lax.broadcasted_iota(
        jnp.int32, (count, count), 0
    )
    same = block_ids[..., :, None] == block_ids[..., None, :]
    return jnp.sum(jnp.logical_and(same, earlier).astype(jnp.int32), axis=-1)


def most_rows_of(tok_rows, adapters):
    return max(2, 2 * tok_rows // adapters)


def body_any(activations, adapter_ids, base_weight, shrink_weight, expand_weight):
    row_ids = adapter_ids[:, 0]
    tok_rows = activations.shape[0]
    feat_part = activations.shape[1]
    output_slice = expand_weight.shape[2]
    out_cols = base_weight.shape[1]
    n_adapt = lax.axis_size("adapter")
    local_count = shrink_weight.shape[0]
    most_rows = most_rows_of(tok_rows, local_count * n_adapt)
    resident_slot_list = local_count * most_rows
    all_slots = n_adapt * resident_slot_list
    home_slot = row_ids * most_rows + ranks_of(row_ids)
    home_map = (
        lax.broadcasted_iota(jnp.int32, (all_slots, tok_rows), 0) == home_slot[None, :]
    ).astype(jnp.bfloat16)
    base_part = jnp.dot(
        lax.all_gather(activations, "adapter", axis=0, tiled=True),
        base_weight,
        preferred_element_type=jnp.float32,
    )
    outgoing = jnp.dot(home_map, activations, preferred_element_type=jnp.float32).astype(
        jnp.bfloat16
    )
    outgoing = outgoing.reshape(n_adapt, resident_slot_list, feat_part)
    arrived = lax.all_to_all(outgoing, "adapter", split_axis=0, concat_axis=0, tiled=True)
    sender_slots = arrived.shape[0]
    grouped = arrived.reshape(sender_slots, local_count, most_rows, feat_part)
    partial_rank = jnp.einsum(
        "sjrd,jdk->sjrk", grouped, shrink_weight, preferred_element_type=jnp.float32
    )
    shrunk = lax.psum(partial_rank, "tensor").astype(jnp.bfloat16)
    expanded_rows = jnp.einsum(
        "sjrk,jkn->sjrn", shrunk, expand_weight, preferred_element_type=jnp.float32
    )
    final_outputs = (
        (adapter_scale_factor * expanded_rows)
        .astype(jnp.bfloat16)
        .reshape(sender_slots, resident_slot_list, output_slice)
    )
    returned = lax.all_to_all(final_outputs, "adapter", split_axis=0, concat_axis=0, tiled=True)
    delta = jnp.einsum(
        "st,sd->td",
        home_map,
        returned.reshape(all_slots, output_slice),
        preferred_element_type=jnp.float32,
    )
    base_blocks = base_part.reshape(n_adapt, tok_rows, out_cols)
    moved = lax.all_to_all(base_blocks, "adapter", split_axis=0, concat_axis=2, tiled=True)
    moved = moved.reshape(tok_rows, out_cols * n_adapt)
    base = lax.psum_scatter(moved, "tensor", scatter_dimension=1, tiled=True)
    return (base + delta).astype(jnp.bfloat16)


VM = pl.BlockSpec(memory_space=pltpu.VMEM)
F32 = jnp.float32
BF16 = jnp.bfloat16


def slot_kernel(most, ids_ref, row_ref, col_ref):
    ids = ids_ref[...]
    count = ids.shape[1]
    i = lax.broadcasted_iota(jnp.int32, (count, count), 0)
    j = lax.broadcasted_iota(jnp.int32, (count, count), 1)
    wide = jnp.broadcast_to(ids, (count, count))
    tall = jnp.sum(jnp.where(i == j, wide, 0), axis=1, keepdims=True)
    same = wide == tall
    row_ref[...] = ids * most + jnp.sum(
        jnp.where(same & (i < j), 1, 0), axis=0, keepdims=True
    )
    col_ref[...] = tall * most + jnp.sum(
        jnp.where(same & (j < i), 1, 0), axis=1, keepdims=True
    )


def first_kernel(x_ref, s_ref, w_ref, held_ref, p32_ref, p16_ref, sh_ref, sems):
    parts = sems.shape[0]
    step = w_ref.shape[0] // parts

    def copy(i):
        lines = slice(i * step, (i + 1) * step)
        return pltpu.make_async_copy(w_ref.at[lines, :], held_ref.at[lines, :], sems.at[i])

    for i in range(parts):
        copy(i).start()
    sh_ref[...] = lax.dot_general(
        x_ref[...], s_ref[...], (((1,), (1,)), ((), ())), preferred_element_type=F32
    )
    for i in range(parts):
        copy(i).wait()
        lines = slice(i * step, (i + 1) * step)
        part = jnp.dot(x_ref[:, lines], held_ref[lines, :], preferred_element_type=F32)
        if i > 0:
            part = p32_ref[...] + part
        p32_ref[...] = part
        if i == parts - 1:
            p16_ref[...] = part.astype(BF16)


def first_stage(x, w, s_t):
    rows, depth = x.shape
    cols = w.shape[1]
    return pl.pallas_call(
        first_kernel,
        in_specs=[VM, VM, pl.BlockSpec(memory_space=pl.ANY)],
        out_specs=[VM] * 4,
        out_shape=[
            pltpu.VMEM(w.shape, w.dtype),
            jax.ShapeDtypeStruct((rows, cols), F32),
            jax.ShapeDtypeStruct((rows, cols), BF16),
            jax.ShapeDtypeStruct((rows, s_t.shape[0]), F32),
        ],
        scratch_shapes=[pltpu.SemaphoreType.DMA((8,))],
        compiler_params=pltpu.CompilerParams(vmem_limit_bytes=VMEM_LIMIT),
        cost_estimate=pl.CostEstimate(
            flops=2 * rows * depth * cols, bytes_accessed=depth * cols * 2, transcendentals=0
        ),
    )(x, s_t, pltpu.with_memory_space_constraint(w, pltpu.HBM))


def stage_kernel(n_in, keep, *refs):
    x_refs, (w_ref, s_ref), rest = refs[:n_in], refs[n_in : n_in + 2], refs[n_in + 2 :]
    before, (p32_ref, p16_ref, sh_ref) = rest[:-3], rest[-3:]
    x = x_refs[0][...]
    for other in x_refs[1:]:
        x = x + other[...]
    rows = x.shape[0]
    if keep:
        sh_ref[: sh_ref.shape[0] - rows, :] = before[0][...]
    sh_ref[sh_ref.shape[0] - rows :, :] = lax.dot_general(
        x, s_ref[...], (((1,), (1,)), ((), ())), preferred_element_type=F32
    )
    cols = w_ref.shape[1]
    step = 256
    for j in range(0, cols, step):
        part = jnp.dot(x, w_ref[:, j : j + step], preferred_element_type=F32)
        p32_ref[:, j : j + step] = part
        p16_ref[:, j : j + step] = part.astype(BF16)


def stage(xs, w, s_t, before=()):
    rows, depth = xs[0].shape
    cols = w.shape[1]
    kept = rows + sum(b.shape[0] for b in before)
    w = pltpu.with_memory_space_constraint(w, pltpu.VMEM)
    return pl.pallas_call(
        functools.partial(stage_kernel, len(xs), bool(before)),
        in_specs=[VM] * (len(xs) + 2 + len(before)),
        out_specs=[VM, VM, VM],
        out_shape=[
            jax.ShapeDtypeStruct((rows, cols), F32),
            jax.ShapeDtypeStruct((rows, cols), BF16),
            jax.ShapeDtypeStruct((kept, s_t.shape[0]), F32),
        ],
        compiler_params=pltpu.CompilerParams(vmem_limit_bytes=VMEM_LIMIT),
        cost_estimate=pl.CostEstimate(
            flops=2 * rows * depth * cols, bytes_accessed=depth * cols * 2, transcendentals=0
        ),
    )(*xs, w, s_t, *before)


def delta_kernel(k, most, e_ref, *refs):
    slots, mine, other, outs = refs[:k], refs[k], refs[k + 1], refs[k + 2 :]
    local, rank, _ = e_ref.shape
    first = lax.axis_index("adapter") * (local * most)
    rows = slots[0].shape[1]
    slot = lax.broadcasted_iota(jnp.int32, (local * most, rows), 0) + first
    for i in range(k):
        block = slice(i * rows, (i + 1) * rows)
        shrunk = (mine[block, :] + other[block, :]).astype(BF16)
        pick = (slot == slots[i][...]).astype(BF16)
        chosen = jnp.dot(pick, shrunk, preferred_element_type=F32).astype(BF16)
        for j in range(local):
            lines = slice(j * most, (j + 1) * most)
            wide = jnp.dot(
                chosen[lines, j * rank : (j + 1) * rank], e_ref[j], preferred_element_type=F32
            )
            outs[i][lines, :] = (adapter_scale_factor * wide).astype(BF16)


def deltas(e, slots, mine, other, most):
    k = len(slots)
    local, _, width = e.shape
    return pl.pallas_call(
        functools.partial(delta_kernel, k, most),
        in_specs=[VM] * (3 + k),
        out_specs=[VM] * k,
        out_shape=[jax.ShapeDtypeStruct((local * most, width), BF16)] * k,
        compiler_params=pltpu.CompilerParams(vmem_limit_bytes=VMEM_LIMIT),
        cost_estimate=pl.CostEstimate(
            flops=k * 2 * local * most * 64 * width, bytes_accessed=4 << 20, transcendentals=0
        ),
    )(e, *slots, mine, other)


def final_kernel(planes, slot_ref, own32_ref, own16_ref, b1, b2, b3, d0, d1, d2, d3, o_ref, base):
    rows, quarter = own32_ref.shape
    me, half = lax.axis_index("adapter"), lax.axis_index("tensor")
    plane_of = [sum(jnp.where(me == a, p[a], 0) for a in range(4)) for p in planes]
    spots = d0.shape[0]
    slot = slot_ref[...]
    lane = lax.broadcasted_iota(jnp.int32, (rows, spots), 1)
    picks = [(slot == lane + plane_of[k] * spots).astype(BF16) for k in range(4)]
    for q in range(2):
        cols = slice(q * quarter, (q + 1) * quarter)

        @pl.when(plane_of[0] == 2 * half + q)
        def _():
            base[...] = own32_ref[...] + own16_ref[...].astype(F32)

        for k, ref in ((1, b1), (2, b2), (3, b3)):

            @pl.when(plane_of[k] == 2 * half + q)
            def _():
                base[...] = ref[...].astype(F32)

        total = base[...]
        for pick, d in zip(picks, (d0, d1, d2, d3)):
            total = total + jnp.dot(pick, d[:, cols], preferred_element_type=F32)
        o_ref[:, cols] = total.astype(BF16)


def body_four(activations, adapter_ids, base_weight, shrink_weight, expand_weight):
    rows = activations.shape[0]
    local, _, rank = shrink_weight.shape
    quarter = base_weight.shape[1]
    most = most_rows_of(rows, local * 4)
    both = ("adapter", "tensor")

    def along(x, pairs):
        return lax.ppermute(x, "adapter", pairs)

    held = ((1, 3, 0, 2), (3, 2, 1, 0), (2, 0, 3, 1))

    def back(k):
        return [(a, held[k - 1][a]) for a in range(4)]

    planes = [[h for h in range(4)]]
    for k in (1, 2, 3):
        planes.append([held[k - 1].index(h) for h in range(4)])
    x = activations
    got_a = along(x, [(0, 2), (3, 1), (1, 0), (2, 3)])

    slot_row, slot_col = pl.pallas_call(
        functools.partial(slot_kernel, most),
        in_specs=[VM],
        out_specs=[VM, VM],
        out_shape=[
            jax.ShapeDtypeStruct((1, rows), jnp.int32),
            jax.ShapeDtypeStruct((rows, 1), jnp.int32),
        ],
        compiler_params=pltpu.CompilerParams(vmem_limit_bytes=VMEM_LIMIT),
    )(adapter_ids.reshape(1, rows))
    slots = [slot_row]
    for k in (1, 2, 3):
        slots.append(along(slot_row, [(h, a) for a, h in back(k)]))

    s_t = jnp.swapaxes(shrink_weight, 1, 2).reshape(local * rank, -1)
    w, p32_0, p16_0, s_0 = first_stage(x, base_weight, s_t)
    x_later, s_0 = lax.optimization_barrier((x, s_0))
    got_c = along(x_later, [(0, 1), (3, 2), (2, 0), (1, 3)])
    got_b = along(x_later, [(1, 2), (2, 1)])
    got_f = along(got_a, [(1, 0), (2, 3)])

    p32_1, p16_1, s_1 = stage([got_a], w, s_t, [s_0])
    p32_2, p16_2, s_2 = stage([got_f, got_b], w, s_t, [s_1])
    got_c, s_2 = lax.optimization_barrier((got_c, s_2))
    p32_3, p16_3, s_3 = stage([got_c], w, s_t)

    def to_half(p):
        return lax.ppermute(
            p, both, [(2 * a + 1 - a // 2, 2 * a + a // 2) for a in range(4)]
        )

    def home_base(p, k):
        return lax.ppermute(
            p, both, [(2 * a + a // 2, 2 * h + a // 2) for a, h in back(k)]
        )

    def flip(s):
        return lax.ppermute(s, "tensor", [(0, 1), (1, 0)])

    own16 = to_half(p16_0)
    bases = []
    for k, p32, p16 in ((1, p32_1, p16_1), (2, p32_2, p16_2), (3, p32_3, p16_3)):
        bases.append(home_base((p32 + to_half(p16)).astype(BF16), k))

    e = expand_weight
    d_0, d_1, d_2 = deltas(e, slots[0:3], s_2, flip(s_2), most)
    (d_3,) = deltas(e, slots[3:4], s_3, flip(s_3), most)
    d_1, d_2, d_3 = along(d_1, back(1)), along(d_2, back(2)), along(d_3, back(3))

    return pl.pallas_call(
        functools.partial(final_kernel, planes),
        in_specs=[VM] * 10,
        out_specs=VM,
        out_shape=jax.ShapeDtypeStruct((rows, 2 * quarter), BF16),
        scratch_shapes=[pltpu.VMEM((rows, quarter), F32)],
        compiler_params=pltpu.CompilerParams(vmem_limit_bytes=VMEM_LIMIT),
    )(slot_col, p32_0, own16, *bases, d_0, d_1, d_2, d_3)


def solution(mesh):
    in_specs = (
        P(("groups", "adapter", "section"), "tensor"),
        P(("groups", "adapter", "section"), None),
        P("tensor", "adapter"),
        P("adapter", "tensor", None),
        P("adapter", None, "tensor"),
    )
    out_specs = P(("groups", "adapter", "section"), "tensor")
    four = mesh.shape["adapter"] == 4 and mesh.shape["tensor"] == 2
    body = body_four if four else body_any
    return jax.shard_map(body, mesh=mesh, in_specs=in_specs, out_specs=out_specs, check_vma=False)
```

```python
import functools

import jax
import jax.numpy as jnp
from jax import lax
from jax.experimental import pallas as pl
from jax.experimental.pallas import tpu as pltpu
from jax.sharding import PartitionSpec as P

adapter_scale_factor = 0.5
VMEM_LIMIT = 8 * 1024 * 1024


def ranks_of(block_ids):
    count = block_ids.shape[-1]
    earlier = lax.broadcasted_iota(jnp.int32, (count, count), 1) < lax.broadcasted_iota(
        jnp.int32, (count, count), 0
    )
    same = block_ids[..., :, None] == block_ids[..., None, :]
    return jnp.sum(jnp.logical_and(same, earlier).astype(jnp.int32), axis=-1)


def most_rows_of(tok_rows, adapters):
    return max(2, 2 * tok_rows // adapters)


def body_any(activations, adapter_ids, base_weight, shrink_weight, expand_weight):
    row_ids = adapter_ids[:, 0]
    tok_rows = activations.shape[0]
    feat_part = activations.shape[1]
    output_slice = expand_weight.shape[2]
    out_cols = base_weight.shape[1]
    n_adapt = lax.axis_size("adapter")
    local_count = shrink_weight.shape[0]
    most_rows = most_rows_of(tok_rows, local_count * n_adapt)
    resident_slot_list = local_count * most_rows
    all_slots = n_adapt * resident_slot_list
    home_slot = row_ids * most_rows + ranks_of(row_ids)
    home_map = (
        lax.broadcasted_iota(jnp.int32, (all_slots, tok_rows), 0) == home_slot[None, :]
    ).astype(jnp.bfloat16)
    base_part = jnp.dot(
        lax.all_gather(activations, "adapter", axis=0, tiled=True),
        base_weight,
        preferred_element_type=jnp.float32,
    )
    outgoing = jnp.dot(home_map, activations, preferred_element_type=jnp.float32).astype(
        jnp.bfloat16
    )
    outgoing = outgoing.reshape(n_adapt, resident_slot_list, feat_part)
    arrived = lax.all_to_all(outgoing, "adapter", split_axis=0, concat_axis=0, tiled=True)
    sender_slots = arrived.shape[0]
    grouped = arrived.reshape(sender_slots, local_count, most_rows, feat_part)
    partial_rank = jnp.einsum(
        "sjrd,jdk->sjrk", grouped, shrink_weight, preferred_element_type=jnp.float32
    )
    shrunk = lax.psum(partial_rank, "tensor").astype(jnp.bfloat16)
    expanded_rows = jnp.einsum(
        "sjrk,jkn->sjrn", shrunk, expand_weight, preferred_element_type=jnp.float32
    )
    final_outputs = (
        (adapter_scale_factor * expanded_rows)
        .astype(jnp.bfloat16)
        .reshape(sender_slots, resident_slot_list, output_slice)
    )
    returned = lax.all_to_all(final_outputs, "adapter", split_axis=0, concat_axis=0, tiled=True)
    delta = jnp.einsum(
        "st,sd->td",
        home_map,
        returned.reshape(all_slots, output_slice),
        preferred_element_type=jnp.float32,
    )
    base_blocks = base_part.reshape(n_adapt, tok_rows, out_cols)
    moved = lax.all_to_all(base_blocks, "adapter", split_axis=0, concat_axis=2, tiled=True)
    moved = moved.reshape(tok_rows, out_cols * n_adapt)
    base = lax.psum_scatter(moved, "tensor", scatter_dimension=1, tiled=True)
    return (base + delta).astype(jnp.bfloat16)


VM = pl.BlockSpec(memory_space=pltpu.VMEM)
HB = pl.BlockSpec(memory_space=pl.ANY)
F32 = jnp.float32
BF16 = jnp.bfloat16
LANES = 128
PARAMS = pltpu.CompilerParams(vmem_limit_bytes=VMEM_LIMIT)


def hbm(x):
    return pltpu.with_memory_space_constraint(x, pltpu.HBM)


def vmem(x):
    return pltpu.with_memory_space_constraint(x, pltpu.VMEM)


def cost(flops, nbytes):
    return pl.CostEstimate(flops=flops, bytes_accessed=nbytes, transcendentals=0)


def pack_kernel(most, ids_ref, x_ref, packed_ref, col_ref, sem):
    depth = x_ref.shape[1]
    copy = pltpu.make_async_copy(x_ref, packed_ref.at[:, :depth], sem)
    copy.start()
    ids = ids_ref[...]
    count = ids.shape[1]
    i = lax.broadcasted_iota(jnp.int32, (count, count), 0)
    j = lax.broadcasted_iota(jnp.int32, (count, count), 1)
    wide = jnp.broadcast_to(ids, (count, count))
    tall = jnp.sum(jnp.where(i == j, wide, 0), axis=1, keepdims=True)
    col = tall * most + jnp.sum(jnp.where((wide == tall) & (j < i), 1, 0), axis=1, keepdims=True)
    col_ref[...] = col
    packed_ref[:, depth:] = jnp.broadcast_to(col.astype(F32), (count, LANES)).astype(BF16)
    copy.wait()


def shrink(x_ref_tail, sums, most, local, rank):
    rows = sums.shape[0]
    slot = x_ref_tail[:, 0:1].astype(F32)
    i = lax.broadcasted_iota(jnp.int32, (rows, rows), 0)
    j = lax.broadcasted_iota(jnp.int32, (rows, rows), 1)
    line = jnp.sum(jnp.where(i == j, slot, 0.0), axis=0, keepdims=True).astype(jnp.int32)
    spots = local * most
    first = lax.axis_index("adapter") * spots
    want = lax.broadcasted_iota(jnp.int32, (spots, rows), 0) + first
    chosen = jnp.dot(
        (want == line).astype(F32),
        sums,
        preferred_element_type=F32,
        precision=lax.Precision.HIGHEST,
    )
    return [
        chosen[k * most : (k + 1) * most, k * rank : (k + 1) * rank] for k in range(local)
    ]


def put_shrunk(parts, top, send_ref, own_ref, most, rank):
    rows = own_ref.shape[0]
    wide = send_ref.shape[1]
    at = wide - LANES
    for k, part in enumerate(parts):
        lines = slice(k * most, (k + 1) * most)
        own_ref[lines, :] = part
        high = part.astype(BF16)
        low = (part - high.astype(F32)).astype(BF16)
        send_ref[top + k * most : top + (k + 1) * most, at:] = jnp.concatenate([high, low], axis=1)
    send_ref[top + rows :, at:] = jnp.zeros((send_ref.shape[0] - top - rows, LANES), BF16)


def put_base(total, top, send_ref, keep_ref):
    rows, width = keep_ref.shape
    half = lax.axis_index("tensor")
    for c in range(2):

        @pl.when(half == c)
        def _():
            keep_ref[...] = total[:, c * width : (c + 1) * width]
            send_ref[top : top + rows, :width] = total[
                :, (1 - c) * width : (2 - c) * width
            ].astype(BF16)


def first_kernel(
    dims, x_ref, s_hbm, w_hbm, w_ref, s_ref, send_ref, keep_ref, own_ref, total, sems
):
    most, local, rank = dims
    parts = sems.shape[0] - 1
    step = w_hbm.shape[0] // parts
    copies = []
    for i in range(parts):
        lines = slice(i * step, (i + 1) * step)
        copies.append(
            pltpu.make_async_copy(w_hbm.at[lines, :], w_ref.at[lines, :], sems.at[i])
        )
        copies[i].start()
    down = pltpu.make_async_copy(s_hbm, s_ref, sems.at[parts])
    down.start()
    for i in range(parts):
        copies[i].wait()
        lines = slice(i * step, (i + 1) * step)
        part = jnp.dot(x_ref[:, lines], w_ref[lines, :], preferred_element_type=F32)
        total[...] = part if i == 0 else total[...] + part
    down.wait()
    depth = w_ref.shape[0]
    sums = lax.dot_general(
        x_ref[:, :depth], s_ref[...], (((1,), (1,)), ((), ())), preferred_element_type=F32
    )
    chosen = shrink(x_ref[:, depth:], sums, most, local, rank)
    put_shrunk(chosen, 0, send_ref, own_ref, most, rank)
    put_base(total, 0, send_ref, keep_ref)


def stage_kernel(dims, n_in, keep_first, *refs):
    most, local, rank = dims
    x_refs, (w_ref, s_ref) = refs[:n_in], refs[n_in : n_in + 2]
    before, (send_ref, keep_ref, own_ref, total) = refs[n_in + 2 : -4], refs[-4:]
    depth = w_ref.shape[0]
    x, tail = x_refs[0][:, :depth], x_refs[0][:, depth:]
    for other in x_refs[1:]:
        x, tail = x + other[:, :depth], tail + other[:, depth:]
    top = 0
    if keep_first:
        top = before[0].shape[0]
        send_ref[:top, :] = before[0][...]
    sums = lax.dot_general(
        x, s_ref[...], (((1,), (1,)), ((), ())), preferred_element_type=F32
    )
    for j in range(0, w_ref.shape[1], 256):
        cols = slice(j, j + 256)
        total[:, cols] = jnp.dot(x, w_ref[:, cols], preferred_element_type=F32)
    put_shrunk(shrink(tail, sums, most, local, rank), top, send_ref, own_ref, most, rank)
    put_base(total, top, send_ref, keep_ref)


def stage_shapes(rows, sent_rows, cols, spots, rank):
    return [
        pltpu.VMEM((sent_rows, cols // 2 + LANES), BF16),
        pltpu.VMEM((rows, cols // 2), F32),
        pltpu.VMEM((spots, rank), F32),
    ]


def first_stage(dims, x, s_t, w):
    rows = x.shape[0]
    depth, cols = w.shape
    most, local, rank = dims
    return pl.pallas_call(
        functools.partial(first_kernel, dims),
        in_specs=[VM, HB, HB],
        out_specs=[VM] * 5,
        out_shape=[pltpu.VMEM(w.shape, BF16), pltpu.VMEM(s_t.shape, BF16)]
        + stage_shapes(rows, rows, cols, local * most, rank),
        scratch_shapes=[pltpu.VMEM((rows, cols), F32), pltpu.SemaphoreType.DMA((9,))],
        compiler_params=PARAMS,
        cost_estimate=cost(2 * rows * depth * cols, depth * cols * 2),
    )(vmem(x), hbm(s_t), hbm(w))


def stage(dims, xs, w, s_t, before=()):
    rows = xs[0].shape[0]
    depth, cols = w.shape
    most, local, rank = dims
    sent = rows + sum(b.shape[0] for b in before)
    return pl.pallas_call(
        functools.partial(stage_kernel, dims, len(xs), bool(before)),
        in_specs=[VM] * (len(xs) + 2 + len(before)),
        out_specs=[VM] * 3,
        out_shape=stage_shapes(rows, sent, cols, local * most, rank),
        scratch_shapes=[pltpu.VMEM((rows, cols), F32)],
        compiler_params=PARAMS,
        cost_estimate=cost(2 * rows * depth * cols, depth * cols * 2),
    )(*xs, vmem(w), vmem(s_t), *before)


def join_kernel(k, got_ref, e_ref, *refs):
    ins, outs = refs[: 2 * k], refs[2 * k :]
    local, rank, _ = e_ref.shape
    width = got_ref.shape[1] - LANES
    rows = got_ref.shape[0] // k
    for i in range(k):
        keep, own, base, delta = ins[2 * i], ins[2 * i + 1], outs[2 * i], outs[2 * i + 1]
        lines = slice(i * rows, (i + 1) * rows)
        spots = own.shape[0]
        most = spots // local
        terms = got_ref[i * rows : i * rows + spots, width:].astype(F32)
        total = (own[...] + terms[:, :rank] + terms[:, rank : 2 * rank]).astype(BF16)
        base[...] = (keep[...] + got_ref[lines, :width].astype(F32)).astype(BF16)
        for j in range(local):
            put = slice(j * most, (j + 1) * most)
            wide = jnp.dot(total[put], e_ref[j], preferred_element_type=F32)
            delta[put, :] = (adapter_scale_factor * wide).astype(BF16)


def join(got, e, pairs):
    k = len(pairs)
    shapes = []
    for keep, own in pairs:
        shapes += [
            pltpu.VMEM(keep.shape, BF16),
            pltpu.VMEM((own.shape[0], e.shape[2]), BF16),
        ]
    return pl.pallas_call(
        functools.partial(join_kernel, k),
        in_specs=[VM] * (2 + 2 * k),
        out_specs=[VM] * (2 * k),
        out_shape=shapes,
        compiler_params=PARAMS,
        cost_estimate=cost(1 << 28, 4 << 20),
    )(got, e, *[a for pair in pairs for a in pair])


def final_kernel(planes, slot_ref, *refs):
    straight, crossed, d_refs = refs[0:4], refs[4:8], refs[8:12]
    o_ref, base = refs[12:]
    rows, width = straight[0].shape
    me, half = lax.axis_index("adapter"), lax.axis_index("tensor")
    plane_of = [sum(jnp.where(me == a, p[a], 0) for a in range(4)) for p in planes]
    spots = d_refs[0].shape[0]
    slot = slot_ref[...]
    lane = lax.broadcasted_iota(jnp.int32, (rows, spots), 1)
    picks = [(slot == lane + plane_of[k] * spots).astype(BF16) for k in range(4)]
    for q in range(2):
        for k in range(4):

            @pl.when(plane_of[k] == 2 * half + q)
            def _():
                base[2 * q] = straight[k][...]
                base[2 * q + 1] = crossed[k][...]

    for q in range(2):
        for c in range(2):
            cols = slice((2 * q + c) * width, (2 * q + c + 1) * width)
            term = jnp.where(half == c, base[2 * q].astype(F32), base[2 * q + 1].astype(F32))
            for pick, d in zip(picks, d_refs):
                term = term + jnp.dot(pick, d[:, cols], preferred_element_type=F32)
            o_ref[:, cols] = term.astype(BF16)


def body_four(activations, adapter_ids, base_weight, shrink_weight, expand_weight):
    rows, depth = activations.shape
    local, _, rank = shrink_weight.shape
    cols = base_weight.shape[1]
    most = most_rows_of(rows, local * 4)
    dims = (most, local, rank)
    both = ("adapter", "tensor")

    def along(x, pairs):
        return lax.ppermute(x, "adapter", pairs)

    held = ((1, 3, 0, 2), (3, 2, 1, 0), (2, 0, 3, 1))

    def back(k):
        return [(a, held[k - 1][a] if k else a) for a in range(4)]

    planes = [list(range(4))]
    for k in (1, 2, 3):
        planes.append([held[k - 1].index(h) for h in range(4)])

    packed, slot_col = pl.pallas_call(
        functools.partial(pack_kernel, most),
        in_specs=[VM, HB],
        out_specs=[VM, VM],
        out_shape=[
            pltpu.VMEM((rows, depth + LANES), BF16),
            jax.ShapeDtypeStruct((rows, 1), jnp.int32),
        ],
        scratch_shapes=[pltpu.SemaphoreType.DMA],
        compiler_params=PARAMS,
    )(adapter_ids.reshape(1, rows), hbm(activations))

    got_a = along(packed, [(0, 2), (3, 1), (1, 0), (2, 3)])
    s_t = jnp.swapaxes(shrink_weight, 1, 2).reshape(local * rank, -1)
    w, s_t, send_0, keep_0, own_0 = first_stage(dims, packed, s_t, base_weight)
    packed, own_0 = lax.optimization_barrier((packed, own_0))
    got_b = along(packed, [(1, 2), (2, 1)])
    got_f = along(got_a, [(1, 0), (2, 3)])

    def flip(s):
        return lax.ppermute(s, "tensor", [(0, 1), (1, 0)])

    def home(base, k):
        straight = [(2 * a + a // 2, 2 * h + a // 2) for a, h in back(k)]
        crossed = [(2 * a + 1 - a // 2, 2 * h + a // 2) for a, h in back(k)]
        return (
            lax.ppermute(base, both, straight) if k else base,
            lax.ppermute(base, both, crossed),
        )

    e = expand_weight
    send_1, keep_1, own_1 = stage(dims, [got_a], w, s_t, [send_0])
    packed, send_1 = lax.optimization_barrier((packed, send_1))
    got_c = along(packed, [(0, 1), (3, 2), (2, 0), (1, 3)])
    base_0, d_0, base_1, d_1 = join(flip(send_1), e, [(keep_0, own_0), (keep_1, own_1)])
    got_b, d_1 = lax.optimization_barrier((got_b, d_1))
    send_2, keep_2, own_2 = stage(dims, [got_f, got_b], w, s_t)
    base_2, d_2 = join(flip(send_2), e, [(keep_2, own_2)])
    got_c, keep_2 = lax.optimization_barrier((got_c, keep_2))
    send_3, keep_3, own_3 = stage(dims, [got_c], w, s_t)
    base_3, d_3 = join(flip(send_3), e, [(keep_3, own_3)])
    ways = [home(b, k) for k, b in enumerate((base_0, base_1, base_2, base_3))]
    d_1, d_2, d_3 = along(d_1, back(1)), along(d_2, back(2)), along(d_3, back(3))

    return pl.pallas_call(
        functools.partial(final_kernel, planes),
        in_specs=[VM] * 13,
        out_specs=VM,
        out_shape=jax.ShapeDtypeStruct((rows, 2 * cols), BF16),
        scratch_shapes=[pltpu.VMEM((4, rows, cols // 2), BF16)],
        compiler_params=PARAMS,
    )(slot_col, *[u for u, _ in ways], *[v for _, v in ways], d_0, d_1, d_2, d_3)


def solution(mesh):
    in_specs = (
        P(("groups", "adapter", "section"), "tensor"),
        P(("groups", "adapter", "section"), None),
        P("tensor", "adapter"),
        P("adapter", "tensor", None),
        P("adapter", None, "tensor"),
    )
    out_specs = P(("groups", "adapter", "section"), "tensor")
    four = mesh.shape["adapter"] == 4 and mesh.shape["tensor"] == 2
    body = body_four if four else body_any
    return jax.shard_map(body, mesh=mesh, in_specs=in_specs, out_specs=out_specs, check_vma=False)
```

```python
import functools

import jax
import jax.numpy as jnp
from jax import lax
from jax.experimental import pallas as pl
from jax.experimental.pallas import tpu as pltpu
from jax.sharding import PartitionSpec as P

adapter_scale_factor = 0.5
VMEM_LIMIT = 8 * 1024 * 1024


def ranks_of(block_ids):
    count = block_ids.shape[-1]
    earlier = lax.broadcasted_iota(jnp.int32, (count, count), 1) < lax.broadcasted_iota(
        jnp.int32, (count, count), 0
    )
    same = block_ids[..., :, None] == block_ids[..., None, :]
    return jnp.sum(jnp.logical_and(same, earlier).astype(jnp.int32), axis=-1)


def most_rows_of(tok_rows, adapters):
    return max(2, 2 * tok_rows // adapters)


def body_any(activations, adapter_ids, base_weight, shrink_weight, expand_weight):
    row_ids = adapter_ids[:, 0]
    tok_rows = activations.shape[0]
    feat_part = activations.shape[1]
    output_slice = expand_weight.shape[2]
    out_cols = base_weight.shape[1]
    n_adapt = lax.axis_size("adapter")
    local_count = shrink_weight.shape[0]
    most_rows = most_rows_of(tok_rows, local_count * n_adapt)
    resident_slot_list = local_count * most_rows
    all_slots = n_adapt * resident_slot_list
    home_slot = row_ids * most_rows + ranks_of(row_ids)
    home_map = (
        lax.broadcasted_iota(jnp.int32, (all_slots, tok_rows), 0) == home_slot[None, :]
    ).astype(jnp.bfloat16)
    base_part = jnp.dot(
        lax.all_gather(activations, "adapter", axis=0, tiled=True),
        base_weight,
        preferred_element_type=jnp.float32,
    )
    outgoing = jnp.dot(home_map, activations, preferred_element_type=jnp.float32).astype(
        jnp.bfloat16
    )
    outgoing = outgoing.reshape(n_adapt, resident_slot_list, feat_part)
    arrived = lax.all_to_all(outgoing, "adapter", split_axis=0, concat_axis=0, tiled=True)
    sender_slots = arrived.shape[0]
    grouped = arrived.reshape(sender_slots, local_count, most_rows, feat_part)
    partial_rank = jnp.einsum(
        "sjrd,jdk->sjrk", grouped, shrink_weight, preferred_element_type=jnp.float32
    )
    shrunk = lax.psum(partial_rank, "tensor").astype(jnp.bfloat16)
    expanded_rows = jnp.einsum(
        "sjrk,jkn->sjrn", shrunk, expand_weight, preferred_element_type=jnp.float32
    )
    final_outputs = (
        (adapter_scale_factor * expanded_rows)
        .astype(jnp.bfloat16)
        .reshape(sender_slots, resident_slot_list, output_slice)
    )
    returned = lax.all_to_all(final_outputs, "adapter", split_axis=0, concat_axis=0, tiled=True)
    delta = jnp.einsum(
        "st,sd->td",
        home_map,
        returned.reshape(all_slots, output_slice),
        preferred_element_type=jnp.float32,
    )
    base_blocks = base_part.reshape(n_adapt, tok_rows, out_cols)
    moved = lax.all_to_all(base_blocks, "adapter", split_axis=0, concat_axis=2, tiled=True)
    moved = moved.reshape(tok_rows, out_cols * n_adapt)
    base = lax.psum_scatter(moved, "tensor", scatter_dimension=1, tiled=True)
    return (base + delta).astype(jnp.bfloat16)


VM = pl.BlockSpec(memory_space=pltpu.VMEM)
HB = pl.BlockSpec(memory_space=pl.ANY)
F32 = jnp.float32
BF16 = jnp.bfloat16
LANES = 128
PARAMS = pltpu.CompilerParams(vmem_limit_bytes=VMEM_LIMIT)


def hbm(x):
    return pltpu.with_memory_space_constraint(x, pltpu.HBM)


def vmem(x):
    return pltpu.with_memory_space_constraint(x, pltpu.VMEM)


def cost(flops, nbytes):
    return pl.CostEstimate(flops=flops, bytes_accessed=nbytes, transcendentals=0)


def pack_kernel(most, ids_ref, x_ref, packed_ref, col_ref, sem):
    depth = x_ref.shape[1]
    copy = pltpu.make_async_copy(x_ref, packed_ref.at[:, :depth], sem)
    copy.start()
    ids = ids_ref[...]
    count = ids.shape[1]
    i = lax.broadcasted_iota(jnp.int32, (count, count), 0)
    j = lax.broadcasted_iota(jnp.int32, (count, count), 1)
    wide = jnp.broadcast_to(ids, (count, count))
    tall = jnp.sum(jnp.where(i == j, wide, 0), axis=1, keepdims=True)
    col = tall * most + jnp.sum(jnp.where((wide == tall) & (j < i), 1, 0), axis=1, keepdims=True)
    col_ref[...] = col
    packed_ref[:, depth:] = jnp.broadcast_to(col.astype(F32), (count, LANES)).astype(BF16)
    copy.wait()


def shrink(x_ref_tail, sums, most, local, rank):
    rows = sums.shape[0]
    slot = x_ref_tail[:, 0:1].astype(F32)
    i = lax.broadcasted_iota(jnp.int32, (rows, rows), 0)
    j = lax.broadcasted_iota(jnp.int32, (rows, rows), 1)
    line = jnp.sum(jnp.where(i == j, slot, 0.0), axis=0, keepdims=True).astype(jnp.int32)
    spots = local * most
    first = lax.axis_index("adapter") * spots
    want = lax.broadcasted_iota(jnp.int32, (spots, rows), 0) + first
    chosen = jnp.dot(
        (want == line).astype(F32),
        sums,
        preferred_element_type=F32,
        precision=lax.Precision.HIGHEST,
    )
    return [
        chosen[k * most : (k + 1) * most, k * rank : (k + 1) * rank] for k in range(local)
    ]


def put_shrunk(parts, top, send_ref, own_ref, most, rank):
    rows = own_ref.shape[0]
    wide = send_ref.shape[1]
    at = wide - LANES
    for k, part in enumerate(parts):
        lines = slice(k * most, (k + 1) * most)
        own_ref[lines, :] = part
        high = part.astype(BF16)
        low = (part - high.astype(F32)).astype(BF16)
        send_ref[top + k * most : top + (k + 1) * most, at:] = jnp.concatenate([high, low], axis=1)
    send_ref[top + rows :, at:] = jnp.zeros((send_ref.shape[0] - top - rows, LANES), BF16)


def put_base(total, top, send_ref, keep_ref):
    rows, width = keep_ref.shape
    half = lax.axis_index("tensor")
    for c in range(2):

        @pl.when(half == c)
        def _():
            keep_ref[...] = total[:, c * width : (c + 1) * width]
            send_ref[top : top + rows, :width] = total[
                :, (1 - c) * width : (2 - c) * width
            ].astype(BF16)


def first_kernel(
    dims, x_ref, s_hbm, w_hbm, w_ref, s_ref, send_ref, keep_ref, own_ref, total, sems
):
    most, local, rank = dims
    parts = sems.shape[0] - 1
    step = w_hbm.shape[0] // parts
    copies = []
    for i in range(parts):
        lines = slice(i * step, (i + 1) * step)
        copies.append(
            pltpu.make_async_copy(w_hbm.at[lines, :], w_ref.at[lines, :], sems.at[i])
        )
        copies[i].start()
    down = pltpu.make_async_copy(s_hbm, s_ref, sems.at[parts])
    down.start()
    for i in range(parts):
        copies[i].wait()
        lines = slice(i * step, (i + 1) * step)
        part = jnp.dot(x_ref[:, lines], w_ref[lines, :], preferred_element_type=F32)
        total[...] = part if i == 0 else total[...] + part
    down.wait()
    depth = w_ref.shape[0]
    sums = lax.dot_general(
        x_ref[:, :depth], s_ref[...], (((1,), (1,)), ((), ())), preferred_element_type=F32
    )
    chosen = shrink(x_ref[:, depth:], sums, most, local, rank)
    put_shrunk(chosen, 0, send_ref, own_ref, most, rank)
    put_base(total, 0, send_ref, keep_ref)


def stage_kernel(dims, n_in, keep_first, *refs):
    most, local, rank = dims
    x_refs, (w_ref, s_ref) = refs[:n_in], refs[n_in : n_in + 2]
    before, (send_ref, keep_ref, own_ref, total) = refs[n_in + 2 : -4], refs[-4:]
    depth = w_ref.shape[0]
    x, tail = x_refs[0][:, :depth], x_refs[0][:, depth:]
    for other in x_refs[1:]:
        x, tail = x + other[:, :depth], tail + other[:, depth:]
    top = 0
    if keep_first:
        top = before[0].shape[0]
        send_ref[:top, :] = before[0][...]
    sums = lax.dot_general(
        x, s_ref[...], (((1,), (1,)), ((), ())), preferred_element_type=F32
    )
    for j in range(0, w_ref.shape[1], 256):
        cols = slice(j, j + 256)
        total[:, cols] = jnp.dot(x, w_ref[:, cols], preferred_element_type=F32)
    put_shrunk(shrink(tail, sums, most, local, rank), top, send_ref, own_ref, most, rank)
    put_base(total, top, send_ref, keep_ref)


def stage_shapes(rows, sent_rows, cols, spots, rank):
    return [
        pltpu.VMEM((sent_rows, cols // 2 + LANES), BF16),
        pltpu.VMEM((rows, cols // 2), F32),
        pltpu.VMEM((spots, rank), F32),
    ]


def first_stage(dims, x, s_t, w):
    rows = x.shape[0]
    depth, cols = w.shape
    most, local, rank = dims
    return pl.pallas_call(
        functools.partial(first_kernel, dims),
        in_specs=[VM, HB, HB],
        out_specs=[VM] * 5,
        out_shape=[pltpu.VMEM(w.shape, BF16), pltpu.VMEM(s_t.shape, BF16)]
        + stage_shapes(rows, rows, cols, local * most, rank),
        scratch_shapes=[pltpu.VMEM((rows, cols), F32), pltpu.SemaphoreType.DMA((9,))],
        compiler_params=PARAMS,
        cost_estimate=cost(1, 1),
    )(vmem(x), hbm(s_t), hbm(w))


def stage(dims, xs, w, s_t, before=()):
    rows = xs[0].shape[0]
    depth, cols = w.shape
    most, local, rank = dims
    sent = rows + sum(b.shape[0] for b in before)
    return pl.pallas_call(
        functools.partial(stage_kernel, dims, len(xs), bool(before)),
        in_specs=[VM] * (len(xs) + 2 + len(before)),
        out_specs=[VM] * 3,
        out_shape=stage_shapes(rows, sent, cols, local * most, rank),
        scratch_shapes=[pltpu.VMEM((rows, cols), F32)],
        compiler_params=PARAMS,
        cost_estimate=cost(1, 1),
    )(*xs, vmem(w), vmem(s_t), *before)


def join_kernel(k, n_mix, got_ref, e_ref, *refs):
    ins, mixed, outs = refs[: 2 * k], refs[2 * k : 2 * k + n_mix], refs[2 * k + n_mix :]
    local, rank, _ = e_ref.shape
    width = got_ref.shape[1] - LANES
    rows = got_ref.shape[0] // k
    owner = lax.axis_index("adapter") // 2 == lax.axis_index("tensor")
    for i in range(k):
        keep, own, delta = ins[2 * i], ins[2 * i + 1], outs[i]
        lines = slice(i * rows, (i + 1) * rows)
        spots = own.shape[0]
        most = spots // local
        terms = got_ref[i * rows : i * rows + spots, width:].astype(F32)
        total = (own[...] + terms[:, :rank] + terms[:, rank : 2 * rank]).astype(BF16)
        base = (keep[...] + got_ref[lines, :width].astype(F32)).astype(BF16)
        if n_mix:
            outs[k][...] = jnp.where(owner, mixed[0][...], base)
            outs[k + 1][...] = jnp.where(owner, base, mixed[0][...])
        else:
            outs[k + i][...] = base
        for j in range(local):
            put = slice(j * most, (j + 1) * most)
            wide = jnp.dot(total[put], e_ref[j], preferred_element_type=F32)
            delta[put, :] = (adapter_scale_factor * wide).astype(BF16)


def join(got, e, pairs, mix=()):
    k = len(pairs)
    keep, own = pairs[0]
    wide = pltpu.VMEM((own.shape[0], e.shape[2]), BF16)
    return pl.pallas_call(
        functools.partial(join_kernel, k, len(mix)),
        in_specs=[VM] * (2 + 2 * k + len(mix)),
        out_specs=[VM] * (2 * k + len(mix)),
        out_shape=[wide] * k + [pltpu.VMEM(keep.shape, BF16)] * (k + len(mix)),
        compiler_params=PARAMS,
        cost_estimate=cost(1, 1),
    )(got, e, *[a for pair in pairs for a in pair], *mix)


def final_kernel(planes, slot_ref, *refs):
    own, by_02, by_13, by_31, by_2 = refs[0:5]
    straight, crossed = (own, by_13, by_02, by_31), (by_02, by_31, by_2, by_13)
    d_refs, (o_ref, base) = refs[5:9], refs[9:]
    rows, width = straight[0].shape
    me, half = lax.axis_index("adapter"), lax.axis_index("tensor")
    plane_of = [sum(jnp.where(me == a, p[a], 0) for a in range(4)) for p in planes]
    spots = d_refs[0].shape[0]
    slot = slot_ref[...]
    lane = lax.broadcasted_iota(jnp.int32, (rows, spots), 1)
    picks = [(slot == lane + plane_of[k] * spots).astype(BF16) for k in range(4)]
    for q in range(2):
        for k in range(4):

            @pl.when(plane_of[k] == 2 * half + q)
            def _():
                base[2 * q] = straight[k][...]
                base[2 * q + 1] = crossed[k][...]

    for q in range(2):
        for c in range(2):
            cols = slice((2 * q + c) * width, (2 * q + c + 1) * width)
            term = jnp.where(half == c, base[2 * q].astype(F32), base[2 * q + 1].astype(F32))
            for pick, d in zip(picks, d_refs):
                term = term + jnp.dot(pick, d[:, cols], preferred_element_type=F32)
            o_ref[:, cols] = term.astype(BF16)


def body_four(activations, adapter_ids, base_weight, shrink_weight, expand_weight):
    rows, depth = activations.shape
    local, _, rank = shrink_weight.shape
    cols = base_weight.shape[1]
    most = most_rows_of(rows, local * 4)
    dims = (most, local, rank)
    both = ("adapter", "tensor")

    def along(x, pairs):
        return lax.ppermute(x, "adapter", pairs)

    held = ((1, 3, 0, 2), (3, 2, 1, 0), (2, 0, 3, 1))

    def back(k):
        return [(a, held[k - 1][a] if k else a) for a in range(4)]

    planes = [list(range(4))]
    for k in (1, 2, 3):
        planes.append([held[k - 1].index(h) for h in range(4)])

    packed, slot_col = pl.pallas_call(
        functools.partial(pack_kernel, most),
        in_specs=[VM, HB],
        out_specs=[VM, VM],
        out_shape=[
            pltpu.VMEM((rows, depth + LANES), BF16),
            jax.ShapeDtypeStruct((rows, 1), jnp.int32),
        ],
        scratch_shapes=[pltpu.SemaphoreType.DMA],
        compiler_params=PARAMS,
    )(adapter_ids.reshape(1, rows), hbm(activations))

    got_a = along(packed, [(0, 2), (3, 1), (1, 0), (2, 3)])
    s_t = jnp.swapaxes(shrink_weight, 1, 2).reshape(local * rank, -1)
    w, s_t, send_0, keep_0, own_0 = first_stage(dims, packed, s_t, base_weight)
    packed, got_a, own_0 = lax.optimization_barrier((packed, got_a, own_0))
    got_f = along(got_a, [(1, 0), (2, 3)])
    got_b = along(packed, [(1, 2), (2, 1)])

    def flip(s):
        return lax.ppermute(s, "tensor", [(0, 1), (1, 0)])

    def straight(k):
        return [(2 * a + a // 2, 2 * h + a // 2) for a, h in back(k)]

    def crossed(k):
        return [(2 * a + 1 - a // 2, 2 * h + a // 2) for a, h in back(k)]

    def home(block, pairs):
        return lax.ppermute(block, both, pairs)

    e = expand_weight
    send_1, keep_1, own_1 = stage(dims, [got_a], w, s_t, [send_0])
    packed, got_f, send_1 = lax.optimization_barrier((packed, got_f, send_1))
    got_c = along(packed, [(0, 1), (3, 2), (2, 0), (1, 3)])
    got_1 = flip(send_1)
    send_2, keep_2, own_2 = stage(dims, [got_f, got_b], w, s_t)
    d_0, d_1, base_0, base_1 = join(got_1, e, [(keep_0, own_0), (keep_1, own_1)])
    came_1 = along(d_1, back(1))
    got_2 = flip(send_2)
    d_2, mix_02, mix_20 = join(got_2, e, [(keep_2, own_2)], [base_0])
    came_2 = along(d_2, back(2))
    got_c, came_1 = lax.optimization_barrier((got_c, came_1))
    send_3, keep_3, own_3 = stage(dims, [got_c], w, s_t)
    send_3, came_2 = lax.optimization_barrier((send_3, came_2))
    d_3, mix_13, mix_31 = join(flip(send_3), e, [(keep_3, own_3)], [base_1])
    from_02 = home(mix_20, straight(2) + crossed(0))
    from_2 = home(mix_02, crossed(2))
    came_3 = along(d_3, back(3))
    from_13 = home(mix_13, straight(1) + crossed(3))
    from_31 = home(mix_31, straight(3) + crossed(1))

    return pl.pallas_call(
        functools.partial(final_kernel, planes),
        in_specs=[VM] * 10,
        out_specs=VM,
        out_shape=jax.ShapeDtypeStruct((rows, 2 * cols), BF16),
        scratch_shapes=[pltpu.VMEM((4, rows, cols // 2), BF16)],
        compiler_params=PARAMS,
    )(slot_col, base_0, from_02, from_13, from_31, from_2, d_0, came_1, came_2, came_3)


def solution(mesh):
    in_specs = (
        P(("groups", "adapter", "section"), "tensor"),
        P(("groups", "adapter", "section"), None),
        P("tensor", "adapter"),
        P("adapter", "tensor", None),
        P("adapter", None, "tensor"),
    )
    out_specs = P(("groups", "adapter", "section"), "tensor")
    four = mesh.shape["adapter"] == 4 and mesh.shape["tensor"] == 2
    body = body_four if four else body_any
    return jax.shard_map(body, mesh=mesh, in_specs=in_specs, out_specs=out_specs, check_vma=False)
```

```python
import functools

import jax
import jax.numpy as jnp
from jax import lax
from jax.experimental import pallas as pl
from jax.experimental.pallas import tpu as pltpu
from jax.sharding import PartitionSpec as P

adapter_scale_factor = 0.5
VMEM_LIMIT = 8 * 1024 * 1024


def ranks_of(block_ids):
    count = block_ids.shape[-1]
    earlier = lax.broadcasted_iota(jnp.int32, (count, count), 1) < lax.broadcasted_iota(
        jnp.int32, (count, count), 0
    )
    same = block_ids[..., :, None] == block_ids[..., None, :]
    return jnp.sum(jnp.logical_and(same, earlier).astype(jnp.int32), axis=-1)


def most_rows_of(tok_rows, adapters):
    return max(2, 2 * tok_rows // adapters)


def body_any(activations, adapter_ids, base_weight, shrink_weight, expand_weight):
    row_ids = adapter_ids[:, 0]
    tok_rows = activations.shape[0]
    feat_part = activations.shape[1]
    output_slice = expand_weight.shape[2]
    out_cols = base_weight.shape[1]
    n_adapt = lax.axis_size("adapter")
    local_count = shrink_weight.shape[0]
    most_rows = most_rows_of(tok_rows, local_count * n_adapt)
    resident_slot_list = local_count * most_rows
    all_slots = n_adapt * resident_slot_list
    home_slot = row_ids * most_rows + ranks_of(row_ids)
    home_map = (
        lax.broadcasted_iota(jnp.int32, (all_slots, tok_rows), 0) == home_slot[None, :]
    ).astype(jnp.bfloat16)
    base_part = jnp.dot(
        lax.all_gather(activations, "adapter", axis=0, tiled=True),
        base_weight,
        preferred_element_type=jnp.float32,
    )
    outgoing = jnp.dot(home_map, activations, preferred_element_type=jnp.float32).astype(
        jnp.bfloat16
    )
    outgoing = outgoing.reshape(n_adapt, resident_slot_list, feat_part)
    arrived = lax.all_to_all(outgoing, "adapter", split_axis=0, concat_axis=0, tiled=True)
    sender_slots = arrived.shape[0]
    grouped = arrived.reshape(sender_slots, local_count, most_rows, feat_part)
    partial_rank = jnp.einsum(
        "sjrd,jdk->sjrk", grouped, shrink_weight, preferred_element_type=jnp.float32
    )
    shrunk = lax.psum(partial_rank, "tensor").astype(jnp.bfloat16)
    expanded_rows = jnp.einsum(
        "sjrk,jkn->sjrn", shrunk, expand_weight, preferred_element_type=jnp.float32
    )
    final_outputs = (
        (adapter_scale_factor * expanded_rows)
        .astype(jnp.bfloat16)
        .reshape(sender_slots, resident_slot_list, output_slice)
    )
    returned = lax.all_to_all(final_outputs, "adapter", split_axis=0, concat_axis=0, tiled=True)
    delta = jnp.einsum(
        "st,sd->td",
        home_map,
        returned.reshape(all_slots, output_slice),
        preferred_element_type=jnp.float32,
    )
    base_blocks = base_part.reshape(n_adapt, tok_rows, out_cols)
    moved = lax.all_to_all(base_blocks, "adapter", split_axis=0, concat_axis=2, tiled=True)
    moved = moved.reshape(tok_rows, out_cols * n_adapt)
    base = lax.psum_scatter(moved, "tensor", scatter_dimension=1, tiled=True)
    return (base + delta).astype(jnp.bfloat16)


VM = pl.BlockSpec(memory_space=pltpu.VMEM)
HB = pl.BlockSpec(memory_space=pl.ANY)
F32 = jnp.float32
BF16 = jnp.bfloat16
LANES = 128
PARAMS = pltpu.CompilerParams(vmem_limit_bytes=VMEM_LIMIT)


def hbm(x):
    return pltpu.with_memory_space_constraint(x, pltpu.HBM)


def vmem(x):
    return pltpu.with_memory_space_constraint(x, pltpu.VMEM)


def cost(flops, nbytes):
    return pl.CostEstimate(flops=flops, bytes_accessed=nbytes, transcendentals=0)


def pack_kernel(most, ids_ref, x_ref, packed_ref, col_ref, sem):
    depth = x_ref.shape[1]
    copy = pltpu.make_async_copy(x_ref, packed_ref.at[:, :depth], sem)
    copy.start()
    ids = ids_ref[...]
    count = ids.shape[1]
    i = lax.broadcasted_iota(jnp.int32, (count, count), 0)
    j = lax.broadcasted_iota(jnp.int32, (count, count), 1)
    wide = jnp.broadcast_to(ids, (count, count))
    tall = jnp.sum(jnp.where(i == j, wide, 0), axis=1, keepdims=True)
    col = tall * most + jnp.sum(jnp.where((wide == tall) & (j < i), 1, 0), axis=1, keepdims=True)
    col_ref[...] = col
    packed_ref[:, depth:] = jnp.broadcast_to(col.astype(F32), (count, LANES)).astype(BF16)
    copy.wait()


def shrink(x_ref_tail, sums, most, local, rank):
    rows = sums.shape[0]
    slot = x_ref_tail[:, 0:1].astype(F32)
    i = lax.broadcasted_iota(jnp.int32, (rows, rows), 0)
    j = lax.broadcasted_iota(jnp.int32, (rows, rows), 1)
    line = jnp.sum(jnp.where(i == j, slot, 0.0), axis=0, keepdims=True).astype(jnp.int32)
    spots = local * most
    first = lax.axis_index("adapter") * spots
    want = lax.broadcasted_iota(jnp.int32, (spots, rows), 0) + first
    chosen = jnp.dot(
        (want == line).astype(F32),
        sums,
        preferred_element_type=F32,
        precision=lax.Precision.HIGHEST,
    )
    return [
        chosen[k * most : (k + 1) * most, k * rank : (k + 1) * rank] for k in range(local)
    ]


def put_shrunk(parts, top, send_ref, own_ref, most, rank):
    rows = own_ref.shape[0]
    wide = send_ref.shape[1]
    at = wide - LANES
    for k, part in enumerate(parts):
        lines = slice(k * most, (k + 1) * most)
        own_ref[lines, :] = part
        high = part.astype(BF16)
        low = (part - high.astype(F32)).astype(BF16)
        send_ref[top + k * most : top + (k + 1) * most, at:] = jnp.concatenate([high, low], axis=1)
    send_ref[top + rows :, at:] = jnp.zeros((send_ref.shape[0] - top - rows, LANES), BF16)


def put_base(total, top, send_ref, keep_ref):
    rows, width = keep_ref.shape
    half = lax.axis_index("tensor")
    for c in range(2):

        @pl.when(half == c)
        def _():
            keep_ref[...] = total[:, c * width : (c + 1) * width]
            send_ref[top : top + rows, :width] = total[
                :, (1 - c) * width : (2 - c) * width
            ].astype(BF16)


def first_kernel(
    dims, x_ref, s_hbm, w_hbm, w_ref, s_ref, send_ref, keep_ref, own_ref, total, sems
):
    most, local, rank = dims
    parts = sems.shape[0] - 1
    step = w_hbm.shape[0] // parts
    copies = []
    for i in range(parts):
        lines = slice(i * step, (i + 1) * step)
        copies.append(
            pltpu.make_async_copy(w_hbm.at[lines, :], w_ref.at[lines, :], sems.at[i])
        )
        copies[i].start()
    down = pltpu.make_async_copy(s_hbm, s_ref, sems.at[parts])
    down.start()
    for i in range(parts):
        copies[i].wait()
        lines = slice(i * step, (i + 1) * step)
        part = jnp.dot(x_ref[:, lines], w_ref[lines, :], preferred_element_type=F32)
        total[...] = part if i == 0 else total[...] + part
    down.wait()
    depth = w_ref.shape[0]
    sums = lax.dot_general(
        x_ref[:, :depth], s_ref[...], (((1,), (1,)), ((), ())), preferred_element_type=F32
    )
    chosen = shrink(x_ref[:, depth:], sums, most, local, rank)
    put_shrunk(chosen, 0, send_ref, own_ref, most, rank)
    put_base(total, 0, send_ref, keep_ref)


def stage_kernel(dims, n_in, keep_first, *refs):
    most, local, rank = dims
    x_refs, (w_ref, s_ref) = refs[:n_in], refs[n_in : n_in + 2]
    before, (send_ref, keep_ref, own_ref, total) = refs[n_in + 2 : -4], refs[-4:]
    depth = w_ref.shape[0]
    x, tail = x_refs[0][:, :depth], x_refs[0][:, depth:]
    for other in x_refs[1:]:
        x, tail = x + other[:, :depth], tail + other[:, depth:]
    top = 0
    if keep_first:
        top = before[0].shape[0]
        send_ref[:top, :] = before[0][...]
    sums = lax.dot_general(
        x, s_ref[...], (((1,), (1,)), ((), ())), preferred_element_type=F32
    )
    for j in range(0, w_ref.shape[1], 256):
        cols = slice(j, j + 256)
        total[:, cols] = jnp.dot(x, w_ref[:, cols], preferred_element_type=F32)
    put_shrunk(shrink(tail, sums, most, local, rank), top, send_ref, own_ref, most, rank)
    put_base(total, top, send_ref, keep_ref)


def stage_shapes(rows, sent_rows, cols, spots, rank):
    return [
        pltpu.VMEM((sent_rows, cols // 2 + LANES), BF16),
        pltpu.VMEM((rows, cols // 2), F32),
        pltpu.VMEM((spots, rank), F32),
    ]


def first_stage(dims, x, s_t, w):
    rows = x.shape[0]
    depth, cols = w.shape
    most, local, rank = dims
    return pl.pallas_call(
        functools.partial(first_kernel, dims),
        in_specs=[VM, HB, HB],
        out_specs=[VM] * 5,
        out_shape=[pltpu.VMEM(w.shape, BF16), pltpu.VMEM(s_t.shape, BF16)]
        + stage_shapes(rows, rows, cols, local * most, rank),
        scratch_shapes=[pltpu.VMEM((rows, cols), F32), pltpu.SemaphoreType.DMA((9,))],
        compiler_params=PARAMS,
        cost_estimate=cost(1, 1),
    )(vmem(x), hbm(s_t), hbm(w))


def stage(dims, xs, w, s_t, before=()):
    rows = xs[0].shape[0]
    depth, cols = w.shape
    most, local, rank = dims
    sent = rows + sum(b.shape[0] for b in before)
    return pl.pallas_call(
        functools.partial(stage_kernel, dims, len(xs), bool(before)),
        in_specs=[VM] * (len(xs) + 2 + len(before)),
        out_specs=[VM] * 3,
        out_shape=stage_shapes(rows, sent, cols, local * most, rank),
        scratch_shapes=[pltpu.VMEM((rows, cols), F32)],
        compiler_params=PARAMS,
        cost_estimate=cost(1, 1),
    )(*xs, vmem(w), vmem(s_t), *before)


def join_kernel(k, n_mix, got_ref, e_ref, *refs):
    ins, mixed, outs = refs[: 2 * k], refs[2 * k : 2 * k + n_mix], refs[2 * k + n_mix :]
    local, rank, _ = e_ref.shape
    width = got_ref.shape[1] - LANES
    rows = got_ref.shape[0] // k
    owner = lax.axis_index("adapter") // 2 == lax.axis_index("tensor")
    for i in range(k):
        keep, own, delta = ins[2 * i], ins[2 * i + 1], outs[i]
        lines = slice(i * rows, (i + 1) * rows)
        spots = own.shape[0]
        most = spots // local
        terms = got_ref[i * rows : i * rows + spots, width:].astype(F32)
        total = (own[...] + terms[:, :rank] + terms[:, rank : 2 * rank]).astype(BF16)
        base = (keep[...] + got_ref[lines, :width].astype(F32)).astype(BF16)
        if n_mix:
            outs[k][...] = jnp.where(owner, mixed[0][...], base)
            outs[k + 1][...] = jnp.where(owner, base, mixed[0][...])
        else:
            outs[k + i][...] = base
        for j in range(local):
            put = slice(j * most, (j + 1) * most)
            wide = jnp.dot(total[put], e_ref[j], preferred_element_type=F32)
            delta[put, :] = (adapter_scale_factor * wide).astype(BF16)


def join(got, e, pairs, mix=()):
    k = len(pairs)
    keep, own = pairs[0]
    wide = pltpu.VMEM((own.shape[0], e.shape[2]), BF16)
    return pl.pallas_call(
        functools.partial(join_kernel, k, len(mix)),
        in_specs=[VM] * (2 + 2 * k + len(mix)),
        out_specs=[VM] * (2 * k + len(mix)),
        out_shape=[wide] * k + [pltpu.VMEM(keep.shape, BF16)] * (k + len(mix)),
        compiler_params=PARAMS,
        cost_estimate=cost(1, 1),
    )(got, e, *[a for pair in pairs for a in pair], *mix)


def final_kernel(planes, slot_ref, *refs):
    own, by_02, by_13, by_31, by_2 = refs[0:5]
    straight, crossed = (own, by_13, by_02, by_31), (by_02, by_31, by_2, by_13)
    d_refs, (o_ref, base) = refs[5:9], refs[9:]
    rows, width = straight[0].shape
    me, half = lax.axis_index("adapter"), lax.axis_index("tensor")
    plane_of = [sum(jnp.where(me == a, p[a], 0) for a in range(4)) for p in planes]
    spots = d_refs[0].shape[0]
    slot = slot_ref[...]
    lane = lax.broadcasted_iota(jnp.int32, (rows, spots), 1)
    picks = [(slot == lane + plane_of[k] * spots).astype(BF16) for k in range(4)]
    for q in range(2):
        for k in range(4):

            @pl.when(plane_of[k] == 2 * half + q)
            def _():
                base[2 * q] = straight[k][...]
                base[2 * q + 1] = crossed[k][...]

    for q in range(2):
        for c in range(2):
            cols = slice((2 * q + c) * width, (2 * q + c + 1) * width)
            term = jnp.where(half == c, base[2 * q].astype(F32), base[2 * q + 1].astype(F32))
            for pick, d in zip(picks, d_refs):
                term = term + jnp.dot(pick, d[:, cols], preferred_element_type=F32)
            o_ref[:, cols] = term.astype(BF16)


def body_four(activations, adapter_ids, base_weight, shrink_weight, expand_weight):
    rows, depth = activations.shape
    local, _, rank = shrink_weight.shape
    cols = base_weight.shape[1]
    most = most_rows_of(rows, local * 4)
    dims = (most, local, rank)
    both = ("adapter", "tensor")

    def along(x, pairs):
        return lax.ppermute(x, "adapter", pairs)

    held = ((1, 3, 0, 2), (3, 2, 1, 0), (2, 0, 3, 1))

    def back(k):
        return [(a, held[k - 1][a] if k else a) for a in range(4)]

    planes = [list(range(4))]
    for k in (1, 2, 3):
        planes.append([held[k - 1].index(h) for h in range(4)])

    packed, slot_col = pl.pallas_call(
        functools.partial(pack_kernel, most),
        in_specs=[VM, HB],
        out_specs=[VM, VM],
        out_shape=[
            pltpu.VMEM((rows, depth + LANES), BF16),
            jax.ShapeDtypeStruct((rows, 1), jnp.int32),
        ],
        scratch_shapes=[pltpu.SemaphoreType.DMA],
        compiler_params=PARAMS,
    )(adapter_ids.reshape(1, rows), hbm(activations))

    got_a = along(packed, [(0, 2), (3, 1), (1, 0), (2, 3)])
    s_t = jnp.swapaxes(shrink_weight, 1, 2).reshape(local * rank, -1)
    w, s_t, send_0, keep_0, own_0 = first_stage(dims, packed, s_t, base_weight)
    packed, got_a, own_0 = lax.optimization_barrier((packed, got_a, own_0))
    got_f = along(got_a, [(1, 0), (2, 3)])
    got_b = along(packed, [(1, 2), (2, 1)])

    def flip(s):
        return lax.ppermute(s, "tensor", [(0, 1), (1, 0)])

    def straight(k):
        return [(2 * a + a // 2, 2 * h + a // 2) for a, h in back(k)]

    def crossed(k):
        return [(2 * a + 1 - a // 2, 2 * h + a // 2) for a, h in back(k)]

    def home(block, pairs):
        return lax.ppermute(block, both, pairs)

    e = expand_weight
    send_1, keep_1, own_1 = stage(dims, [got_a], w, s_t, [send_0])
    packed, got_f, send_1 = lax.optimization_barrier((packed, got_f, send_1))
    got_c = along(packed, [(0, 1), (3, 2), (2, 0), (1, 3)])
    got_1 = flip(send_1)
    send_2, keep_2, own_2 = stage(dims, [got_f, got_b], w, s_t)
    d_0, d_1, base_0, base_1 = join(got_1, e, [(keep_0, own_0), (keep_1, own_1)])
    came_1 = along(d_1, back(1))
    got_2 = flip(send_2)
    d_2, mix_02, mix_20 = join(got_2, e, [(keep_2, own_2)], [base_0])
    came_2 = along(d_2, back(2))
    got_c, _ = lax.optimization_barrier((got_c, d_2))
    send_3, keep_3, own_3 = stage(dims, [got_c], w, s_t)
    got_3, came_1 = lax.optimization_barrier((flip(send_3), came_1))
    d_3, mix_13, mix_31 = join(got_3, e, [(keep_3, own_3)], [base_1])
    from_02 = home(mix_20, straight(2) + crossed(0))
    from_2 = home(mix_02, crossed(2))
    came_3 = along(d_3, back(3))
    from_13 = home(mix_13, straight(1) + crossed(3))
    from_31 = home(mix_31, straight(3) + crossed(1))

    return pl.pallas_call(
        functools.partial(final_kernel, planes),
        in_specs=[VM] * 10,
        out_specs=VM,
        out_shape=jax.ShapeDtypeStruct((rows, 2 * cols), BF16),
        scratch_shapes=[pltpu.VMEM((4, rows, cols // 2), BF16)],
        compiler_params=PARAMS,
    )(slot_col, base_0, from_02, from_13, from_31, from_2, d_0, came_1, came_2, came_3)


def solution(mesh):
    in_specs = (
        P(("groups", "adapter", "section"), "tensor"),
        P(("groups", "adapter", "section"), None),
        P("tensor", "adapter"),
        P("adapter", "tensor", None),
        P("adapter", None, "tensor"),
    )
    out_specs = P(("groups", "adapter", "section"), "tensor")
    four = mesh.shape["adapter"] == 4 and mesh.shape["tensor"] == 2
    body = body_four if four else body_any
    return jax.shard_map(body, mesh=mesh, in_specs=in_specs, out_specs=out_specs, check_vma=False)
```

```python
import functools

import jax
import jax.numpy as jnp
from jax import lax
from jax.experimental import pallas as pl
from jax.experimental.pallas import tpu as pltpu
from jax.sharding import PartitionSpec as P

adapter_scale_factor = 0.5
VMEM_LIMIT = 8 * 1024 * 1024


def ranks_of(block_ids):
    count = block_ids.shape[-1]
    earlier = lax.broadcasted_iota(jnp.int32, (count, count), 1) < lax.broadcasted_iota(
        jnp.int32, (count, count), 0
    )
    same = block_ids[..., :, None] == block_ids[..., None, :]
    return jnp.sum(jnp.logical_and(same, earlier).astype(jnp.int32), axis=-1)


def most_rows_of(tok_rows, adapters):
    return max(2, 2 * tok_rows // adapters)


def body_any(activations, adapter_ids, base_weight, shrink_weight, expand_weight):
    row_ids = adapter_ids[:, 0]
    tok_rows = activations.shape[0]
    feat_part = activations.shape[1]
    output_slice = expand_weight.shape[2]
    out_cols = base_weight.shape[1]
    n_adapt = lax.axis_size("adapter")
    local_count = shrink_weight.shape[0]
    most_rows = most_rows_of(tok_rows, local_count * n_adapt)
    resident_slot_list = local_count * most_rows
    all_slots = n_adapt * resident_slot_list
    home_slot = row_ids * most_rows + ranks_of(row_ids)
    home_map = (
        lax.broadcasted_iota(jnp.int32, (all_slots, tok_rows), 0) == home_slot[None, :]
    ).astype(jnp.bfloat16)
    base_part = jnp.dot(
        lax.all_gather(activations, "adapter", axis=0, tiled=True),
        base_weight,
        preferred_element_type=jnp.float32,
    )
    outgoing = jnp.dot(home_map, activations, preferred_element_type=jnp.float32).astype(
        jnp.bfloat16
    )
    outgoing = outgoing.reshape(n_adapt, resident_slot_list, feat_part)
    arrived = lax.all_to_all(outgoing, "adapter", split_axis=0, concat_axis=0, tiled=True)
    sender_slots = arrived.shape[0]
    grouped = arrived.reshape(sender_slots, local_count, most_rows, feat_part)
    partial_rank = jnp.einsum(
        "sjrd,jdk->sjrk", grouped, shrink_weight, preferred_element_type=jnp.float32
    )
    shrunk = lax.psum(partial_rank, "tensor").astype(jnp.bfloat16)
    expanded_rows = jnp.einsum(
        "sjrk,jkn->sjrn", shrunk, expand_weight, preferred_element_type=jnp.float32
    )
    final_outputs = (
        (adapter_scale_factor * expanded_rows)
        .astype(jnp.bfloat16)
        .reshape(sender_slots, resident_slot_list, output_slice)
    )
    returned = lax.all_to_all(final_outputs, "adapter", split_axis=0, concat_axis=0, tiled=True)
    delta = jnp.einsum(
        "st,sd->td",
        home_map,
        returned.reshape(all_slots, output_slice),
        preferred_element_type=jnp.float32,
    )
    base_blocks = base_part.reshape(n_adapt, tok_rows, out_cols)
    moved = lax.all_to_all(base_blocks, "adapter", split_axis=0, concat_axis=2, tiled=True)
    moved = moved.reshape(tok_rows, out_cols * n_adapt)
    base = lax.psum_scatter(moved, "tensor", scatter_dimension=1, tiled=True)
    return (base + delta).astype(jnp.bfloat16)


VM = pl.BlockSpec(memory_space=pltpu.VMEM)
HB = pl.BlockSpec(memory_space=pl.ANY)
F32 = jnp.float32
BF16 = jnp.bfloat16
LANES = 128
PARAMS = pltpu.CompilerParams(vmem_limit_bytes=VMEM_LIMIT)


def hbm(x):
    return pltpu.with_memory_space_constraint(x, pltpu.HBM)


def vmem(x):
    return pltpu.with_memory_space_constraint(x, pltpu.VMEM)


def cost(flops, nbytes):
    return pl.CostEstimate(flops=flops, bytes_accessed=nbytes, transcendentals=0)


def pack_kernel(most, ids_hbm, x_ref, packed_ref, col_ref, ids_ref, sems):
    depth = x_ref.shape[1]
    copy = pltpu.make_async_copy(x_ref, packed_ref.at[:, :depth], sems.at[0])
    fetch = pltpu.make_async_copy(ids_hbm, ids_ref, sems.at[1])
    fetch.start()
    copy.start()
    fetch.wait()
    ids = ids_ref[...]
    count = ids.shape[1]
    i = lax.broadcasted_iota(jnp.int32, (count, count), 0)
    j = lax.broadcasted_iota(jnp.int32, (count, count), 1)
    wide = jnp.broadcast_to(ids, (count, count))
    tall = jnp.sum(jnp.where(i == j, wide, 0), axis=1, keepdims=True)
    col = tall * most + jnp.sum(jnp.where((wide == tall) & (j < i), 1, 0), axis=1, keepdims=True)
    col_ref[...] = col
    packed_ref[:, depth:] = jnp.broadcast_to(col.astype(F32), (count, LANES)).astype(BF16)
    copy.wait()


def shrink(x_ref_tail, sums, most, local, rank):
    rows = sums.shape[0]
    slot = x_ref_tail[:, 0:1].astype(F32)
    i = lax.broadcasted_iota(jnp.int32, (rows, rows), 0)
    j = lax.broadcasted_iota(jnp.int32, (rows, rows), 1)
    line = jnp.sum(jnp.where(i == j, slot, 0.0), axis=0, keepdims=True).astype(jnp.int32)
    spots = local * most
    first = lax.axis_index("adapter") * spots
    want = lax.broadcasted_iota(jnp.int32, (spots, rows), 0) + first
    chosen = jnp.dot(
        (want == line).astype(F32),
        sums,
        preferred_element_type=F32,
        precision=lax.Precision.HIGHEST,
    )
    return [
        chosen[k * most : (k + 1) * most, k * rank : (k + 1) * rank] for k in range(local)
    ]


def put_shrunk(parts, top, send_ref, own_ref, most, rank):
    rows = own_ref.shape[0]
    wide = send_ref.shape[1]
    at = wide - LANES
    for k, part in enumerate(parts):
        lines = slice(k * most, (k + 1) * most)
        own_ref[lines, :] = part
        high = part.astype(BF16)
        low = (part - high.astype(F32)).astype(BF16)
        send_ref[top + k * most : top + (k + 1) * most, at:] = jnp.concatenate([high, low], axis=1)
    send_ref[top + rows :, at:] = jnp.zeros((send_ref.shape[0] - top - rows, LANES), BF16)


def put_base(total, top, send_ref, keep_ref):
    rows, width = keep_ref.shape
    half = lax.axis_index("tensor")
    for c in range(2):

        @pl.when(half == c)
        def _():
            keep_ref[...] = total[:, c * width : (c + 1) * width]
            send_ref[top : top + rows, :width] = total[
                :, (1 - c) * width : (2 - c) * width
            ].astype(BF16)


def first_kernel(
    dims, x_ref, s_hbm, w_hbm, w_ref, s_ref, send_ref, keep_ref, own_ref, total, sems
):
    most, local, rank = dims
    parts = sems.shape[0] - 1
    step = w_hbm.shape[0] // parts
    copies = []
    for i in range(parts):
        lines = slice(i * step, (i + 1) * step)
        copies.append(
            pltpu.make_async_copy(w_hbm.at[lines, :], w_ref.at[lines, :], sems.at[i])
        )
        copies[i].start()
    down = pltpu.make_async_copy(s_hbm, s_ref, sems.at[parts])
    down.start()
    for i in range(parts):
        copies[i].wait()
        lines = slice(i * step, (i + 1) * step)
        part = jnp.dot(x_ref[:, lines], w_ref[lines, :], preferred_element_type=F32)
        total[...] = part if i == 0 else total[...] + part
    down.wait()
    depth = w_ref.shape[0]
    sums = lax.dot_general(
        x_ref[:, :depth], s_ref[...], (((1,), (1,)), ((), ())), preferred_element_type=F32
    )
    chosen = shrink(x_ref[:, depth:], sums, most, local, rank)
    put_shrunk(chosen, 0, send_ref, own_ref, most, rank)
    put_base(total, 0, send_ref, keep_ref)


def stage_kernel(dims, n_in, keep_first, *refs):
    most, local, rank = dims
    x_refs, (w_ref, s_ref) = refs[:n_in], refs[n_in : n_in + 2]
    before, (send_ref, keep_ref, own_ref, total) = refs[n_in + 2 : -4], refs[-4:]
    depth = w_ref.shape[0]
    x, tail = x_refs[0][:, :depth], x_refs[0][:, depth:]
    for other in x_refs[1:]:
        x, tail = x + other[:, :depth], tail + other[:, depth:]
    top = 0
    if keep_first:
        top = before[0].shape[0]
        send_ref[:top, :] = before[0][...]
    sums = lax.dot_general(
        x, s_ref[...], (((1,), (1,)), ((), ())), preferred_element_type=F32
    )
    for j in range(0, w_ref.shape[1], 256):
        cols = slice(j, j + 256)
        total[:, cols] = jnp.dot(x, w_ref[:, cols], preferred_element_type=F32)
    put_shrunk(shrink(tail, sums, most, local, rank), top, send_ref, own_ref, most, rank)
    put_base(total, top, send_ref, keep_ref)


def stage_shapes(rows, sent_rows, cols, spots, rank):
    return [
        pltpu.VMEM((sent_rows, cols // 2 + LANES), BF16),
        pltpu.VMEM((rows, cols // 2), F32),
        pltpu.VMEM((spots, rank), F32),
    ]


def first_stage(dims, x, s_t, w):
    rows = x.shape[0]
    depth, cols = w.shape
    most, local, rank = dims
    return pl.pallas_call(
        functools.partial(first_kernel, dims),
        in_specs=[VM, HB, HB],
        out_specs=[VM] * 5,
        out_shape=[pltpu.VMEM(w.shape, BF16), pltpu.VMEM(s_t.shape, BF16)]
        + stage_shapes(rows, rows, cols, local * most, rank),
        scratch_shapes=[pltpu.VMEM((rows, cols), F32), pltpu.SemaphoreType.DMA((9,))],
        compiler_params=PARAMS,
        cost_estimate=cost(1, 1),
    )(vmem(x), hbm(s_t), hbm(w))


def stage(dims, xs, w, s_t, before=()):
    rows = xs[0].shape[0]
    depth, cols = w.shape
    most, local, rank = dims
    sent = rows + sum(b.shape[0] for b in before)
    return pl.pallas_call(
        functools.partial(stage_kernel, dims, len(xs), bool(before)),
        in_specs=[VM] * (len(xs) + 2 + len(before)),
        out_specs=[VM] * 3,
        out_shape=stage_shapes(rows, sent, cols, local * most, rank),
        scratch_shapes=[pltpu.VMEM((rows, cols), F32)],
        compiler_params=PARAMS,
        cost_estimate=cost(1, 1),
    )(*xs, vmem(w), vmem(s_t), *before)


def join_kernel(k, n_mix, got_ref, e_ref, *refs):
    ins, mixed, outs = refs[: 2 * k], refs[2 * k : 2 * k + n_mix], refs[2 * k + n_mix :]
    local, rank, _ = e_ref.shape
    width = got_ref.shape[1] - LANES
    rows = got_ref.shape[0] // k
    owner = lax.axis_index("adapter") // 2 == lax.axis_index("tensor")
    for i in range(k):
        keep, own, delta = ins[2 * i], ins[2 * i + 1], outs[i]
        lines = slice(i * rows, (i + 1) * rows)
        spots = own.shape[0]
        most = spots // local
        terms = got_ref[i * rows : i * rows + spots, width:].astype(F32)
        total = (own[...] + terms[:, :rank] + terms[:, rank : 2 * rank]).astype(BF16)
        base = (keep[...] + got_ref[lines, :width].astype(F32)).astype(BF16)
        if n_mix:
            outs[k][...] = jnp.where(owner, mixed[0][...], base)
            outs[k + 1][...] = jnp.where(owner, base, mixed[0][...])
        else:
            outs[k + i][...] = base
        for j in range(local):
            put = slice(j * most, (j + 1) * most)
            wide = jnp.dot(total[put], e_ref[j], preferred_element_type=F32)
            delta[put, :] = (adapter_scale_factor * wide).astype(BF16)


def join(got, e, pairs, mix=()):
    k = len(pairs)
    keep, own = pairs[0]
    wide = pltpu.VMEM((own.shape[0], e.shape[2]), BF16)
    return pl.pallas_call(
        functools.partial(join_kernel, k, len(mix)),
        in_specs=[VM] * (2 + 2 * k + len(mix)),
        out_specs=[VM] * (2 * k + len(mix)),
        out_shape=[wide] * k + [pltpu.VMEM(keep.shape, BF16)] * (k + len(mix)),
        compiler_params=PARAMS,
        cost_estimate=cost(1, 1),
    )(got, e, *[a for pair in pairs for a in pair], *mix)


def final_kernel(planes, slot_ref, *refs):
    own, by_02, by_13, by_31, by_2 = refs[0:5]
    straight, crossed = (own, by_13, by_02, by_31), (by_02, by_31, by_2, by_13)
    d_refs, (o_ref, base) = refs[5:9], refs[9:]
    rows, width = straight[0].shape
    me, half = lax.axis_index("adapter"), lax.axis_index("tensor")
    plane_of = [sum(jnp.where(me == a, p[a], 0) for a in range(4)) for p in planes]
    spots = d_refs[0].shape[0]
    slot = slot_ref[...]
    lane = lax.broadcasted_iota(jnp.int32, (rows, spots), 1)
    picks = [(slot == lane + plane_of[k] * spots).astype(BF16) for k in range(4)]
    for q in range(2):
        for k in range(4):

            @pl.when(plane_of[k] == 2 * half + q)
            def _():
                base[2 * q] = straight[k][...]
                base[2 * q + 1] = crossed[k][...]

    for q in range(2):
        for c in range(2):
            cols = slice((2 * q + c) * width, (2 * q + c + 1) * width)
            term = jnp.where(half == c, base[2 * q].astype(F32), base[2 * q + 1].astype(F32))
            for pick, d in zip(picks, d_refs):
                term = term + jnp.dot(pick, d[:, cols], preferred_element_type=F32)
            o_ref[:, cols] = term.astype(BF16)


def body_four(activations, adapter_ids, base_weight, shrink_weight, expand_weight):
    rows, depth = activations.shape
    local, _, rank = shrink_weight.shape
    cols = base_weight.shape[1]
    most = most_rows_of(rows, local * 4)
    dims = (most, local, rank)
    both = ("adapter", "tensor")

    def along(x, pairs):
        return lax.ppermute(x, "adapter", pairs)

    held = ((1, 3, 0, 2), (3, 2, 1, 0), (2, 0, 3, 1))

    def back(k):
        return [(a, held[k - 1][a] if k else a) for a in range(4)]

    planes = [list(range(4))]
    for k in (1, 2, 3):
        planes.append([held[k - 1].index(h) for h in range(4)])

    packed, slot_col = pl.pallas_call(
        functools.partial(pack_kernel, most),
        in_specs=[HB, HB],
        out_specs=[VM, VM],
        out_shape=[
            pltpu.VMEM((rows, depth + LANES), BF16),
            jax.ShapeDtypeStruct((rows, 1), jnp.int32),
        ],
        scratch_shapes=[pltpu.VMEM((1, rows), jnp.int32), pltpu.SemaphoreType.DMA((2,))],
        compiler_params=PARAMS,
    )(hbm(adapter_ids.reshape(1, rows)), hbm(activations))

    got_a = along(packed, [(0, 2), (3, 1), (1, 0), (2, 3)])
    s_t = jnp.swapaxes(shrink_weight, 1, 2).reshape(local * rank, -1)
    w, s_t, send_0, keep_0, own_0 = first_stage(dims, packed, s_t, base_weight)
    packed, got_a, own_0 = lax.optimization_barrier((packed, got_a, own_0))
    got_f = along(got_a, [(1, 0), (2, 3)])
    got_b = along(packed, [(1, 2), (2, 1)])

    def flip(s):
        return lax.ppermute(s, "tensor", [(0, 1), (1, 0)])

    def straight(k):
        return [(2 * a + a // 2, 2 * h + a // 2) for a, h in back(k)]

    def crossed(k):
        return [(2 * a + 1 - a // 2, 2 * h + a // 2) for a, h in back(k)]

    def home(block, pairs):
        return lax.ppermute(block, both, pairs)

    e = expand_weight
    send_1, keep_1, own_1 = stage(dims, [got_a], w, s_t, [send_0])
    packed, got_f, send_1 = lax.optimization_barrier((packed, got_f, send_1))
    got_c = along(packed, [(0, 1), (3, 2), (2, 0), (1, 3)])
    got_1 = flip(send_1)
    send_2, keep_2, own_2 = stage(dims, [got_f, got_b], w, s_t)
    d_0, d_1, base_0, base_1 = join(got_1, e, [(keep_0, own_0), (keep_1, own_1)])
    came_1 = along(d_1, back(1))
    got_2 = flip(send_2)
    d_2, mix_02, mix_20 = join(got_2, e, [(keep_2, own_2)], [base_0])
    came_2 = along(d_2, back(2))
    got_c, _ = lax.optimization_barrier((got_c, d_2))
    send_3, keep_3, own_3 = stage(dims, [got_c], w, s_t)
    got_3, came_1 = lax.optimization_barrier((flip(send_3), came_1))
    d_3, mix_13, mix_31 = join(got_3, e, [(keep_3, own_3)], [base_1])
    from_02 = home(mix_20, straight(2) + crossed(0))
    from_2 = home(mix_02, crossed(2))
    came_3 = along(d_3, back(3))
    from_13 = home(mix_13, straight(1) + crossed(3))
    from_31 = home(mix_31, straight(3) + crossed(1))

    return pl.pallas_call(
        functools.partial(final_kernel, planes),
        in_specs=[VM] * 10,
        out_specs=VM,
        out_shape=jax.ShapeDtypeStruct((rows, 2 * cols), BF16),
        scratch_shapes=[pltpu.VMEM((4, rows, cols // 2), BF16)],
        compiler_params=PARAMS,
    )(slot_col, base_0, from_02, from_13, from_31, from_2, d_0, came_1, came_2, came_3)


def solution(mesh):
    in_specs = (
        P(("groups", "adapter", "section"), "tensor"),
        P(("groups", "adapter", "section"), None),
        P("tensor", "adapter"),
        P("adapter", "tensor", None),
        P("adapter", None, "tensor"),
    )
    out_specs = P(("groups", "adapter", "section"), "tensor")
    four = mesh.shape["adapter"] == 4 and mesh.shape["tensor"] == 2
    body = body_four if four else body_any
    return jax.shard_map(body, mesh=mesh, in_specs=in_specs, out_specs=out_specs, check_vma=False)
```

```python
import functools

import jax
import jax.numpy as jnp
from jax import lax
from jax.experimental import pallas as pl
from jax.experimental.pallas import tpu as pltpu
from jax.sharding import PartitionSpec as P

adapter_scale_factor = 0.5
VMEM_LIMIT = 8 * 1024 * 1024


def ranks_of(block_ids):
    count = block_ids.shape[-1]
    earlier = lax.broadcasted_iota(jnp.int32, (count, count), 1) < lax.broadcasted_iota(
        jnp.int32, (count, count), 0
    )
    same = block_ids[..., :, None] == block_ids[..., None, :]
    return jnp.sum(jnp.logical_and(same, earlier).astype(jnp.int32), axis=-1)


def most_rows_of(tok_rows, adapters):
    return max(2, 2 * tok_rows // adapters)


def body_any(activations, adapter_ids, base_weight, shrink_weight, expand_weight):
    row_ids = adapter_ids[:, 0]
    tok_rows = activations.shape[0]
    feat_part = activations.shape[1]
    output_slice = expand_weight.shape[2]
    out_cols = base_weight.shape[1]
    n_adapt = lax.axis_size("adapter")
    local_count = shrink_weight.shape[0]
    most_rows = most_rows_of(tok_rows, local_count * n_adapt)
    resident_slot_list = local_count * most_rows
    all_slots = n_adapt * resident_slot_list
    home_slot = row_ids * most_rows + ranks_of(row_ids)
    home_map = (
        lax.broadcasted_iota(jnp.int32, (all_slots, tok_rows), 0) == home_slot[None, :]
    ).astype(jnp.bfloat16)
    base_part = jnp.dot(
        lax.all_gather(activations, "adapter", axis=0, tiled=True),
        base_weight,
        preferred_element_type=jnp.float32,
    )
    outgoing = jnp.dot(home_map, activations, preferred_element_type=jnp.float32).astype(
        jnp.bfloat16
    )
    outgoing = outgoing.reshape(n_adapt, resident_slot_list, feat_part)
    arrived = lax.all_to_all(outgoing, "adapter", split_axis=0, concat_axis=0, tiled=True)
    sender_slots = arrived.shape[0]
    grouped = arrived.reshape(sender_slots, local_count, most_rows, feat_part)
    partial_rank = jnp.einsum(
        "sjrd,jdk->sjrk", grouped, shrink_weight, preferred_element_type=jnp.float32
    )
    shrunk = lax.psum(partial_rank, "tensor").astype(jnp.bfloat16)
    expanded_rows = jnp.einsum(
        "sjrk,jkn->sjrn", shrunk, expand_weight, preferred_element_type=jnp.float32
    )
    final_outputs = (
        (adapter_scale_factor * expanded_rows)
        .astype(jnp.bfloat16)
        .reshape(sender_slots, resident_slot_list, output_slice)
    )
    returned = lax.all_to_all(final_outputs, "adapter", split_axis=0, concat_axis=0, tiled=True)
    delta = jnp.einsum(
        "st,sd->td",
        home_map,
        returned.reshape(all_slots, output_slice),
        preferred_element_type=jnp.float32,
    )
    base_blocks = base_part.reshape(n_adapt, tok_rows, out_cols)
    moved = lax.all_to_all(base_blocks, "adapter", split_axis=0, concat_axis=2, tiled=True)
    moved = moved.reshape(tok_rows, out_cols * n_adapt)
    base = lax.psum_scatter(moved, "tensor", scatter_dimension=1, tiled=True)
    return (base + delta).astype(jnp.bfloat16)


VM = pl.BlockSpec(memory_space=pltpu.VMEM)
HB = pl.BlockSpec(memory_space=pl.ANY)
F32 = jnp.float32
BF16 = jnp.bfloat16
LANES = 128
PARAMS = pltpu.CompilerParams(vmem_limit_bytes=VMEM_LIMIT)


def hbm(x):
    return pltpu.with_memory_space_constraint(x, pltpu.HBM)


def vmem(x):
    return pltpu.with_memory_space_constraint(x, pltpu.VMEM)


def cost(flops, nbytes):
    return pl.CostEstimate(flops=flops, bytes_accessed=nbytes, transcendentals=0)


def pack_kernel(most, ids_ref, x_ref, packed_ref, col_ref, sem):
    depth = x_ref.shape[1]
    copy = pltpu.make_async_copy(x_ref, packed_ref.at[:, :depth], sem)
    copy.start()
    ids = ids_ref[...]
    count = ids.shape[1]
    i = lax.broadcasted_iota(jnp.int32, (count, count), 0)
    j = lax.broadcasted_iota(jnp.int32, (count, count), 1)
    wide = jnp.broadcast_to(ids, (count, count))
    tall = jnp.sum(jnp.where(i == j, wide, 0), axis=1, keepdims=True)
    col = tall * most + jnp.sum(jnp.where((wide == tall) & (j < i), 1, 0), axis=1, keepdims=True)
    col_ref[...] = col
    packed_ref[:, depth:] = jnp.broadcast_to(col.astype(F32), (count, LANES)).astype(BF16)
    copy.wait()


def shrink(x_ref_tail, sums, most, local, rank):
    rows = sums.shape[0]
    slot = x_ref_tail[:, 0:1].astype(F32)
    i = lax.broadcasted_iota(jnp.int32, (rows, rows), 0)
    j = lax.broadcasted_iota(jnp.int32, (rows, rows), 1)
    line = jnp.sum(jnp.where(i == j, slot, 0.0), axis=0, keepdims=True).astype(jnp.int32)
    spots = local * most
    first = lax.axis_index("adapter") * spots
    want = lax.broadcasted_iota(jnp.int32, (spots, rows), 0) + first
    chosen = jnp.dot(
        (want == line).astype(F32),
        sums,
        preferred_element_type=F32,
        precision=lax.Precision.HIGHEST,
    )
    return [
        chosen[k * most : (k + 1) * most, k * rank : (k + 1) * rank] for k in range(local)
    ]


def put_shrunk(parts, top, send_ref, own_ref, most, rank):
    rows = own_ref.shape[0]
    wide = send_ref.shape[1]
    at = wide - LANES
    for k, part in enumerate(parts):
        lines = slice(k * most, (k + 1) * most)
        own_ref[lines, :] = part
        high = part.astype(BF16)
        low = (part - high.astype(F32)).astype(BF16)
        send_ref[top + k * most : top + (k + 1) * most, at:] = jnp.concatenate([high, low], axis=1)
    send_ref[top + rows :, at:] = jnp.zeros((send_ref.shape[0] - top - rows, LANES), BF16)


def put_base(total, top, send_ref, keep_ref):
    rows, width = keep_ref.shape
    half = lax.axis_index("tensor")
    for c in range(2):

        @pl.when(half == c)
        def _():
            keep_ref[...] = total[:, c * width : (c + 1) * width]
            send_ref[top : top + rows, :width] = total[
                :, (1 - c) * width : (2 - c) * width
            ].astype(BF16)


def first_kernel(
    dims, x_ref, s_hbm, w_hbm, w_ref, s_ref, send_ref, keep_ref, own_ref, total, sems
):
    most, local, rank = dims
    parts = sems.shape[0] - 1
    step = w_hbm.shape[0] // parts
    copies = []
    for i in range(parts):
        lines = slice(i * step, (i + 1) * step)
        copies.append(
            pltpu.make_async_copy(w_hbm.at[lines, :], w_ref.at[lines, :], sems.at[i])
        )
        copies[i].start()
    down = pltpu.make_async_copy(s_hbm, s_ref, sems.at[parts])
    down.start()
    for i in range(parts):
        copies[i].wait()
        lines = slice(i * step, (i + 1) * step)
        part = jnp.dot(x_ref[:, lines], w_ref[lines, :], preferred_element_type=F32)
        total[...] = part if i == 0 else total[...] + part
    down.wait()
    depth = w_ref.shape[0]
    sums = lax.dot_general(
        x_ref[:, :depth], s_ref[...], (((1,), (1,)), ((), ())), preferred_element_type=F32
    )
    chosen = shrink(x_ref[:, depth:], sums, most, local, rank)
    put_shrunk(chosen, 0, send_ref, own_ref, most, rank)
    put_base(total, 0, send_ref, keep_ref)


def stage_kernel(dims, n_in, keep_first, *refs):
    most, local, rank = dims
    x_refs, (w_ref, s_ref) = refs[:n_in], refs[n_in : n_in + 2]
    before, (send_ref, keep_ref, own_ref, total) = refs[n_in + 2 : -4], refs[-4:]
    depth = w_ref.shape[0]
    x, tail = x_refs[0][:, :depth], x_refs[0][:, depth:]
    for other in x_refs[1:]:
        x, tail = x + other[:, :depth], tail + other[:, depth:]
    top = 0
    if keep_first:
        top = before[0].shape[0]
        send_ref[:top, :] = before[0][...]
    sums = lax.dot_general(
        x, s_ref[...], (((1,), (1,)), ((), ())), preferred_element_type=F32
    )
    for j in range(0, w_ref.shape[1], 256):
        cols = slice(j, j + 256)
        total[:, cols] = jnp.dot(x, w_ref[:, cols], preferred_element_type=F32)
    put_shrunk(shrink(tail, sums, most, local, rank), top, send_ref, own_ref, most, rank)
    put_base(total, top, send_ref, keep_ref)


def stage_shapes(rows, sent_rows, cols, spots, rank):
    return [
        pltpu.VMEM((sent_rows, cols // 2 + LANES), BF16),
        pltpu.VMEM((rows, cols // 2), F32),
        pltpu.VMEM((spots, rank), F32),
    ]


def first_stage(dims, x, s_t, w):
    rows = x.shape[0]
    depth, cols = w.shape
    most, local, rank = dims
    return pl.pallas_call(
        functools.partial(first_kernel, dims),
        in_specs=[VM, HB, HB],
        out_specs=[VM] * 5,
        out_shape=[pltpu.VMEM(w.shape, BF16), pltpu.VMEM(s_t.shape, BF16)]
        + stage_shapes(rows, rows, cols, local * most, rank),
        scratch_shapes=[pltpu.VMEM((rows, cols), F32), pltpu.SemaphoreType.DMA((9,))],
        compiler_params=PARAMS,
        cost_estimate=cost(1, 1),
    )(vmem(x), hbm(s_t), hbm(w))


def stage(dims, xs, w, s_t, before=()):
    rows = xs[0].shape[0]
    depth, cols = w.shape
    most, local, rank = dims
    sent = rows + sum(b.shape[0] for b in before)
    return pl.pallas_call(
        functools.partial(stage_kernel, dims, len(xs), bool(before)),
        in_specs=[VM] * (len(xs) + 2 + len(before)),
        out_specs=[VM] * 3,
        out_shape=stage_shapes(rows, sent, cols, local * most, rank),
        scratch_shapes=[pltpu.VMEM((rows, cols), F32)],
        compiler_params=PARAMS,
        cost_estimate=cost(1, 1),
    )(*xs, vmem(w), vmem(s_t), *before)


def join_kernel(k, n_mix, got_ref, e_ref, *refs):
    ins, mixed, outs = refs[: 2 * k], refs[2 * k : 2 * k + n_mix], refs[2 * k + n_mix :]
    local, rank, _ = e_ref.shape
    width = got_ref.shape[1] - LANES
    rows = got_ref.shape[0] // k
    owner = lax.axis_index("adapter") // 2 == lax.axis_index("tensor")
    for i in range(k):
        keep, own, delta = ins[2 * i], ins[2 * i + 1], outs[i]
        lines = slice(i * rows, (i + 1) * rows)
        spots = own.shape[0]
        most = spots // local
        terms = got_ref[i * rows : i * rows + spots, width:].astype(F32)
        total = (own[...] + terms[:, :rank] + terms[:, rank : 2 * rank]).astype(BF16)
        base = (keep[...] + got_ref[lines, :width].astype(F32)).astype(BF16)
        if n_mix:
            outs[k][...] = jnp.where(owner, mixed[0][...], base)
            outs[k + 1][...] = jnp.where(owner, base, mixed[0][...])
        else:
            outs[k + i][...] = base
        for j in range(local):
            put = slice(j * most, (j + 1) * most)
            wide = jnp.dot(total[put], e_ref[j], preferred_element_type=F32)
            delta[put, :] = (adapter_scale_factor * wide).astype(BF16)


def join(got, e, pairs, mix=()):
    k = len(pairs)
    keep, own = pairs[0]
    wide = pltpu.VMEM((own.shape[0], e.shape[2]), BF16)
    return pl.pallas_call(
        functools.partial(join_kernel, k, len(mix)),
        in_specs=[VM] * (2 + 2 * k + len(mix)),
        out_specs=[VM] * (2 * k + len(mix)),
        out_shape=[wide] * k + [pltpu.VMEM(keep.shape, BF16)] * (k + len(mix)),
        compiler_params=PARAMS,
        cost_estimate=cost(1, 1),
    )(got, e, *[a for pair in pairs for a in pair], *mix)


def final_kernel(planes, slot_ref, *refs):
    own, by_02, by_13, by_31, by_2 = refs[0:5]
    straight, crossed = (own, by_13, by_02, by_31), (by_02, by_31, by_2, by_13)
    d_refs, (o_ref, base) = refs[5:9], refs[9:]
    rows, width = straight[0].shape
    me, half = lax.axis_index("adapter"), lax.axis_index("tensor")
    plane_of = [sum(jnp.where(me == a, p[a], 0) for a in range(4)) for p in planes]
    spots = d_refs[0].shape[0]
    slot = slot_ref[...]
    lane = lax.broadcasted_iota(jnp.int32, (rows, spots), 1)
    picks = [(slot == lane + plane_of[k] * spots).astype(BF16) for k in range(4)]
    for q in range(2):
        for k in range(4):

            @pl.when(plane_of[k] == 2 * half + q)
            def _():
                base[2 * q] = straight[k][...]
                base[2 * q + 1] = crossed[k][...]

    for q in range(2):
        for c in range(2):
            cols = slice((2 * q + c) * width, (2 * q + c + 1) * width)
            term = jnp.where(half == c, base[2 * q].astype(F32), base[2 * q + 1].astype(F32))
            for pick, d in zip(picks, d_refs):
                term = term + jnp.dot(pick, d[:, cols], preferred_element_type=F32)
            o_ref[:, cols] = term.astype(BF16)


def body_four(activations, adapter_ids, base_weight, shrink_weight, expand_weight):
    rows, depth = activations.shape
    local, _, rank = shrink_weight.shape
    cols = base_weight.shape[1]
    most = most_rows_of(rows, local * 4)
    dims = (most, local, rank)
    both = ("adapter", "tensor")

    def along(x, pairs):
        return lax.ppermute(x, "adapter", pairs)

    held = ((1, 3, 0, 2), (3, 2, 1, 0), (2, 0, 3, 1))

    def back(k):
        return [(a, held[k - 1][a] if k else a) for a in range(4)]

    planes = [list(range(4))]
    for k in (1, 2, 3):
        planes.append([held[k - 1].index(h) for h in range(4)])

    packed, slot_col = pl.pallas_call(
        functools.partial(pack_kernel, most),
        in_specs=[VM, HB],
        out_specs=[VM, VM],
        out_shape=[
            pltpu.VMEM((rows, depth + LANES), BF16),
            jax.ShapeDtypeStruct((rows, 1), jnp.int32),
        ],
        scratch_shapes=[pltpu.SemaphoreType.DMA],
        compiler_params=PARAMS,
    )(adapter_ids.reshape(1, rows), hbm(activations))

    got_a = along(packed, [(0, 2), (3, 1), (1, 0), (2, 3)])
    s_t = jnp.swapaxes(shrink_weight, 1, 2).reshape(local * rank, -1)
    w, s_t, send_0, keep_0, own_0 = first_stage(dims, packed, s_t, base_weight)
    packed, got_a, own_0 = lax.optimization_barrier((packed, got_a, own_0))
    got_f = along(got_a, [(1, 0), (2, 3)])
    got_b = along(packed, [(1, 2), (2, 1)])

    def flip(s):
        return lax.ppermute(s, "tensor", [(0, 1), (1, 0)])

    def straight(k):
        return [(2 * a + a // 2, 2 * h + a // 2) for a, h in back(k)]

    def crossed(k):
        return [(2 * a + 1 - a // 2, 2 * h + a // 2) for a, h in back(k)]

    def home(block, pairs):
        return lax.ppermute(block, both, pairs)

    e = expand_weight
    send_1, keep_1, own_1 = stage(dims, [got_a], w, s_t, [send_0])
    packed, got_f, send_1 = lax.optimization_barrier((packed, got_f, send_1))
    got_c = along(packed, [(0, 1), (3, 2), (2, 0), (1, 3)])
    got_1 = flip(send_1)
    send_2, keep_2, own_2 = stage(dims, [got_f, got_b], w, s_t)
    d_0, d_1, base_0, base_1 = join(got_1, e, [(keep_0, own_0), (keep_1, own_1)])
    came_1 = along(d_1, back(1))
    got_2 = flip(send_2)
    d_2, mix_02, mix_20 = join(got_2, e, [(keep_2, own_2)], [base_0])
    came_2 = along(d_2, back(2))
    got_c, _ = lax.optimization_barrier((got_c, d_2))
    send_3, keep_3, own_3 = stage(dims, [got_c], w, s_t)
    got_3 = flip(send_3)
    d_3, mix_13, mix_31 = join(got_3, e, [(keep_3, own_3)], [base_1])
    from_02 = home(mix_20, straight(2) + crossed(0))
    from_2 = home(mix_02, crossed(2))
    d_3, came_1 = lax.optimization_barrier((d_3, came_1))
    came_3 = along(d_3, back(3))
    from_13 = home(mix_13, straight(1) + crossed(3))
    from_31 = home(mix_31, straight(3) + crossed(1))

    return pl.pallas_call(
        functools.partial(final_kernel, planes),
        in_specs=[VM] * 10,
        out_specs=VM,
        out_shape=jax.ShapeDtypeStruct((rows, 2 * cols), BF16),
        scratch_shapes=[pltpu.VMEM((4, rows, cols // 2), BF16)],
        compiler_params=PARAMS,
    )(slot_col, base_0, from_02, from_13, from_31, from_2, d_0, came_1, came_2, came_3)


def solution(mesh):
    in_specs = (
        P(("groups", "adapter", "section"), "tensor"),
        P(("groups", "adapter", "section"), None),
        P("tensor", "adapter"),
        P("adapter", "tensor", None),
        P("adapter", None, "tensor"),
    )
    out_specs = P(("groups", "adapter", "section"), "tensor")
    four = mesh.shape["adapter"] == 4 and mesh.shape["tensor"] == 2
    body = body_four if four else body_any
    return jax.shard_map(body, mesh=mesh, in_specs=in_specs, out_specs=out_specs, check_vma=False)
```
